32 devices in a mesh: dp: 8 (over z, x), mp: 4 (over y, core).
Axes of the slice: x: 2, y: 2, z: 4, core: 2. Of those that a mesh axis runs over, the one named last changes fastest.
Arguments:
- embeddings: float32 [16384, 1024], P('dp', 'mp'), may hold values from -400 to 400
- cluster_of: int32 [16384], replicated, may hold values from 0 to 1023, as said below
- doc_order: int32 [16384], replicated, may hold values from 0 to 16383, each once
Outputs:
- max_similar: float32 [16384], P('dp')
The draws below stay inside these ranges and needn't reach their ends.
Inputs may be any that keep to these rules, and one draw needn't show every extreme that they name: `cluster_of`: cluster c belongs to owner device c // 32, numbered dp index * (devices along mp) + mp index. Of the rows of one dp block, at most 128 go to one owner, and some owner receives exactly 128 from every block. No cluster holds more than 256 documents, and some cluster holds exactly 256.
All inputs are finite; a program needn't handle non-finite values.
Results may differ from the reference program's by a relative error of at most 0.0003.
Values may be sent and summed in bfloat16 or wider, within the bound.
No kernel may reach another device: no remote copies, remote signals or barrier semaphores. Data moves between devices by JAX's collectives and lax.ppermute only.
A program may use at most 64 MiB of HBM per device.

```python
import math
import jax
import jax.numpy as jnp
from jax import lax

E = 1024
DOC_DEV = 512
CL_DEV = 32
MOST = 256
BAND = 2
DOCS = 16384
CLUSTERS = 1024
N_DP = 8
N_MP = 4
DEVICES = 32


def slot_ranks(owners):
    length = owners.shape[0]
    ordering = jnp.argsort(owners, stable=True)
    ranked = owners[ordering]
    leading = jnp.searchsorted(ranked, ranked, side='left').astype(jnp.int32)
    within = jnp.arange(length, dtype=jnp.int32) - leading
    return jnp.zeros((length,), jnp.int32).at[ordering].set(within)


def build_clusters(key):
    quarter = DOC_DEV // (4 * N_DP)
    block_rows = DOC_DEV * N_MP
    key_perm, key_shift, key_rows = jax.random.split(key, 3)
    placing = jax.random.permutation(key_perm, DEVICES).astype(jnp.int32)
    position = jnp.zeros((DEVICES,), jnp.int32).at[placing].set(jnp.arange(DEVICES, dtype=jnp.int32))
    base_count = quarter * (2 * (position % 4) + 1)
    pair_index = position // 2
    side_sign = 2 * (position % 2) - 1
    shifts = jax.random.randint(key_shift, (N_DP, DEVICES // 2), -quarter, quarter + 1).astype(jnp.int32)
    shifts = shifts.at[:, 1].set(quarter)
    counts = base_count[None, :] + side_sign[None, :] * shifts[:, pair_index]
    bounds = jnp.cumsum(counts, axis=1)
    spot_index = jnp.arange(block_rows, dtype=jnp.int32)
    grouped = jax.vmap(lambda limits: jnp.searchsorted(limits, spot_index, side='right'))(bounds).astype(jnp.int32)
    row_keys = jax.random.split(key_rows, N_DP)
    owners = jax.vmap(lambda one_key, sorted_owners: sorted_owners[jax.random.permutation(one_key, block_rows)])(row_keys, grouped)
    within_block = jax.vmap(slot_ranks)(owners)
    offsets = jnp.cumsum(counts, axis=0) - counts
    owner_loads = jnp.sum(counts, axis=0)
    owner_rank = jnp.take_along_axis(offsets, owners, axis=1) + within_block
    spare_rows = jnp.maximum(owner_loads[owners] - MOST, 1)
    beyond = jnp.maximum(owner_rank - MOST, 0)
    inner_index = 1 + (CL_DEV - 1) * (beyond * beyond + spare_rows * beyond) // (2 * spare_rows * spare_rows)
    inner_index = jnp.where(owner_rank < MOST, 0, inner_index)
    return (owners * CL_DEV + inner_index).reshape(DOCS).astype(jnp.int32)


def draw_cluster_of(key, part):
    return build_clusters(jax.random.fold_in(key, 7))


def draw_embeddings(key, part):
    clusters = build_clusters(jax.random.fold_in(key, 7))
    key_one = jax.random.fold_in(jax.random.fold_in(key, 11), 0)
    key_two = jax.random.fold_in(jax.random.fold_in(key, 11), 1)
    key_three = jax.random.fold_in(jax.random.fold_in(key, 11), 2)
    key_five = jax.random.fold_in(jax.random.fold_in(key, 11), 4)
    centers = jax.random.normal(key_one, (CLUSTERS, E), jnp.float32)
    spread = jnp.exp(jax.random.uniform(key_five, (DOCS, 1), jnp.float32, math.log(0.3), math.log(2.0)))
    noise_part = jax.random.normal(key_two, (DOCS, E), jnp.float32)
    scales = jnp.exp(jax.random.uniform(key_three, (DOCS, 1), jnp.float32, 0.0, math.log(10.0)))
    return (scales * (centers[clusters] + spread * noise_part)).astype(jnp.float32)


def setup_inputs(seed: int = 0) -> dict:
    key_of = jax.random.split(jax.random.key(seed), 4)
    embeddings = draw_embeddings(jax.random.fold_in(key_of[3], 71), 0)
    cluster_of = draw_cluster_of(jax.random.fold_in(key_of[3], 71), 0)
    doc_order = jax.random.permutation(key_of[2], DOCS).astype(jnp.int32)
    return {"embeddings": embeddings, "cluster_of": cluster_of, "doc_order": doc_order}


def band_maxima(unit_rows, clusters, ranks):
    row_count = unit_rows.shape[0]
    blocks = row_count // 128
    tile_rows = unit_rows.reshape(blocks, 128, -1)
    tile_cluster = clusters.reshape(blocks, 128)
    tile_rank = ranks.reshape(blocks, 128)
    highest = jnp.zeros((blocks, 128), jnp.float32)
    for offset_blocks in range(min(BAND, blocks - 1) + 1):
        later_tiles = tile_rows[offset_blocks:]
        early_tiles = tile_rows[:blocks - offset_blocks]
        cosines = jnp.einsum('bie,bje->bij', later_tiles, early_tiles, precision=lax.Precision.HIGHEST)
        same_group = (tile_cluster[offset_blocks:, :, None] == tile_cluster[:blocks - offset_blocks, None, :]) & (tile_rank[:blocks - offset_blocks, None, :] < tile_rank[offset_blocks:, :, None])
        largest = lax.optimization_barrier(jnp.max(jnp.where(same_group, cosines, 0.0), axis=2))
        highest = highest.at[offset_blocks:].max(largest)
    return highest.reshape(row_count)

def reference(embeddings, cluster_of, doc_order):
    sums = lax.optimization_barrier(jnp.sum(embeddings * embeddings, axis=1, keepdims=True))
    unit_rows = (embeddings * lax.rsqrt(sums + 1e-06)).astype(jnp.bfloat16)
    by_rank = jnp.argsort(doc_order, stable=True)
    by_both = by_rank[jnp.argsort(cluster_of[by_rank], stable=True)]
    highest = band_maxima(unit_rows[by_both].astype(jnp.float32), cluster_of[by_both], doc_order[by_both])
    return jnp.zeros((DOCS,), jnp.float32).at[by_both].set(highest)
```

```python
import functools

import jax
import jax.numpy as jnp
from jax import lax
from jax.experimental import pallas as pl
from jax.experimental.pallas import tpu as pltpu
from jax.sharding import PartitionSpec as P

CL_DEV = 32
LANES = 128
F32, BF16, I32 = jnp.float32, jnp.bfloat16, jnp.int32
VMEM = pl.BlockSpec(memory_space=pltpu.VMEM)
SMEM = pl.BlockSpec(memory_space=pltpu.SMEM)


def iota(shape, dimension):
    return lax.broadcasted_iota(I32, shape, dimension)


def dot(a, b):
    return lax.dot_general(a, b, (((1,), (0,)), ((), ())), preferred_element_type=F32)


def dot_nt(a, b):
    return lax.dot_general(a, b, (((1,), (1,)), ((), ())), preferred_element_type=F32)


def column(row):
    return jnp.transpose(jnp.broadcast_to(row, (LANES, LANES)))


def to_bf16(mask):
    return jnp.where(mask, 1.0, 0.0).astype(BF16)


def slot_targets(cluster_rows, owner_count, capacity):
    tiles = cluster_rows.shape[0]
    earlier = to_bf16(iota((LANES, LANES), 0) < iota((LANES, LANES), 1))
    owner_ids = iota((owner_count, LANES), 0)
    carried = jnp.zeros((owner_count, 1), F32)
    targets = []
    for tile in range(tiles):
        owners = cluster_rows[tile : tile + 1, :] // CL_DEV
        mine = owner_ids == owners
        one_hot = to_bf16(mine)
        counted = dot(one_hot, earlier) + carried
        rank = jnp.sum(jnp.where(mine, counted, 0.0), axis=0, keepdims=True)
        carried = carried + jnp.sum(jnp.where(mine, 1.0, 0.0), axis=1, keepdims=True)
        targets.append(owners * capacity + rank.astype(I32))
    return targets


def pack_kernel(owner_count, capacity, place, x_ref, sums_ref, cluster_ref, out_ref, target_ref, rows, picks):
    tiles = x_ref.shape[0] // LANES
    step = picks.shape[0]
    first = pl.multiple_of(place[0] * tiles, 8)
    targets = slot_targets(cluster_ref[pl.ds(first, tiles), :], owner_count, capacity)
    for tile in range(tiles):
        target_ref[tile : tile + 1, :] = targets[tile]
        total = jnp.sum(sums_ref[:, tile, :], axis=0, keepdims=True)
        scale = column(lax.rsqrt(total + 1e-06))
        span = slice(tile * LANES, (tile + 1) * LANES)
        for part in range(x_ref.shape[1] // LANES):
            lanes = slice(part * LANES, (part + 1) * LANES)
            rows[span, lanes] = (x_ref[span, lanes] * scale).astype(BF16)

    slot_ids = iota((LANES, LANES), 0).astype(BF16)

    def fill(index, _):
        for group in range(step // LANES):
            base = (index * (step // LANES) + group) * LANES
            for tile in range(tiles):
                local = target_ref[tile : tile + 1, :] - base
                local = jnp.where((local >= 0) & (local < LANES), local, -1).astype(F32).astype(BF16)
                picks[group * LANES : (group + 1) * LANES, tile * LANES : (tile + 1) * LANES] = jnp.where(
                    slot_ids == local, jnp.ones((), BF16), jnp.zeros((), BF16)
                )
        start = pl.multiple_of(index * step, step)
        out_ref[pl.ds(start, step), :] = dot(picks[...], rows[...]).astype(BF16)
        return 0

    lax.fori_loop(0, out_ref.shape[0] // step, fill, 0)


def keys_kernel(dp_size, capacity, docs, place, cluster_ref, order_ref, row_ref, column_ref):
    tiles = cluster_ref.shape[0]
    block_tiles = tiles // dp_size
    me = place[1]
    mine = (cluster_ref[...] // CL_DEV) == me
    ones = to_bf16(mine)
    within = dot(ones, to_bf16(iota((LANES, LANES), 0) < iota((LANES, LANES), 1)))
    totals = jnp.sum(jnp.where(mine, 1.0, 0.0), axis=1, keepdims=True).astype(BF16)
    tile_row, tile_column = iota((tiles, tiles), 0), iota((tiles, tiles), 1)
    before = to_bf16((tile_column < tile_row) & (tile_column // block_tiles == tile_row // block_tiles))
    rank = within + dot(before, jnp.broadcast_to(totals, (tiles, LANES)))
    blocks_in_group = LANES // capacity
    block_of = iota((tiles, LANES), 0) // block_tiles
    lane = (block_of % blocks_in_group) * capacity + rank.astype(I32)
    lane = jnp.where(mine, lane, -1)
    keys = cluster_ref[...] * docs + order_ref[...] + 1
    group_tiles = block_tiles * blocks_in_group
    slot_ids = iota((LANES, LANES), 0)
    for group in range(tiles // group_tiles):
        total = jnp.zeros((8, LANES), F32)
        for tile in range(group * group_tiles, (group + 1) * group_tiles):
            key = keys[tile : tile + 1, :]
            pieces = [((key >> (8 * piece)) & 255).astype(F32) for piece in range(4)]
            pieces = jnp.concatenate(pieces + [jnp.zeros((4, LANES), F32)], axis=0).astype(BF16)
            hits = to_bf16(slot_ids == lane[tile : tile + 1, :])
            total = total + dot_nt(pieces, hits)
        total = total.astype(I32)
        key = total[0:1] + (total[1:2] << 8) + (total[2:3] << 16) + (total[3:4] << 24) - 1
        row_ref[group : group + 1, :] = key
        column_ref[group * LANES : (group + 1) * LANES, :] = column(key)


def pairs_kernel(docs, arrived_ref, row_ref, column_ref, out_ref):
    dp_size, mp_size, capacity, features = arrived_ref.shape
    slots = dp_size * capacity
    groups = slots // LANES
    blocks = LANES // capacity
    for group in range(groups):
        key = row_ref[group : group + 1, :]
        lowest = jnp.where(key < 0, 0, (key // docs) * docs)
        cosines = jnp.zeros((slots, LANES), F32)
        for part in range(mp_size):
            all_rows = arrived_ref[:, part].reshape(slots, features)
            some_rows = arrived_ref[group * blocks : (group + 1) * blocks, part].reshape(LANES, features)
            cosines = cosines + dot_nt(all_rows, some_rows)
        earlier = column_ref[...]
        good = (earlier >= lowest) & (earlier < key)
        out_ref[group : group + 1, :] = jnp.max(jnp.where(good, cosines, 0.0), axis=0, keepdims=True)


def pick_kernel(capacity, results_ref, target_ref, out_ref):
    owner_count = results_ref.shape[0]
    tiles = target_ref.shape[0]
    results = results_ref[...]
    high = results.astype(BF16)
    rest = results - high.astype(F32)
    middle = rest.astype(BF16)
    low = (rest - middle.astype(F32)).astype(BF16)
    pieces = jnp.concatenate([high, middle, low], axis=0)
    owner_ids = iota((owner_count, LANES), 0)
    rank_ids = iota((results.shape[1], LANES), 0)
    for tile in range(tiles):
        target = target_ref[tile : tile + 1, :]
        owner = target // capacity
        one_hot = to_bf16(owner_ids == owner)
        one_hot = jnp.concatenate([one_hot, one_hot, one_hot], axis=0)
        ranked = lax.dot_general(pieces, one_hot, (((0,), (0,)), ((), ())), preferred_element_type=F32)
        hit = rank_ids == target - owner * capacity
        out_ref[tile : tile + 1, :] = jnp.sum(jnp.where(hit, ranked, 0.0), axis=0, keepdims=True)


def call(kernel, out_shape, specs, scratch=(), cost=0, megabytes=40):
    return pl.pallas_call(
        kernel,
        out_shape=out_shape,
        in_specs=specs,
        out_specs=jax.tree.map(lambda _: VMEM, out_shape),
        scratch_shapes=list(scratch),
        compiler_params=pltpu.CompilerParams(vmem_limit_bytes=megabytes << 20),
        cost_estimate=pl.CostEstimate(flops=cost, bytes_accessed=1 << 20, transcendentals=0),
    )


def shards(embeddings, cluster_of, doc_order):
    block_rows, features = embeddings.shape
    docs = cluster_of.shape[0]
    dp_size, mp_size = lax.axis_size("dp"), lax.axis_size("mp")
    devices = dp_size * mp_size
    capacity = 2 * block_rows // devices
    slots = dp_size * capacity
    tiles = block_rows // LANES
    dp_index, mp_index = lax.axis_index("dp"), lax.axis_index("mp")
    place = jnp.stack([dp_index, dp_index * mp_size + mp_index]).astype(I32)
    clusters = cluster_of.reshape(docs // LANES, LANES)
    orders = doc_order.reshape(docs // LANES, LANES)

    squares = jnp.sum(embeddings * embeddings, axis=1).reshape(tiles, LANES)
    sums = lax.all_gather(squares, "mp")
    shape = jax.ShapeDtypeStruct
    outgoing, targets = call(
        functools.partial(pack_kernel, devices, capacity),
        (shape((devices * capacity, features), BF16), shape((tiles, LANES), I32)),
        [SMEM, VMEM, VMEM, VMEM],
        [pltpu.VMEM((block_rows, features), BF16), pltpu.VMEM((512, block_rows), BF16)],
        2 * devices * capacity * block_rows * features,
    )(place, embeddings, sums, clusters)
    arrived = lax.all_to_all(
        outgoing.reshape(devices, capacity, features), ("dp", "mp"), split_axis=0, concat_axis=0, tiled=True
    )
    key_rows, key_columns = call(
        functools.partial(keys_kernel, dp_size, capacity, docs),
        (shape((slots // LANES, LANES), I32), shape((slots, LANES), I32)),
        [SMEM, VMEM, VMEM],
        cost=10**9,
    )(place, clusters, orders)
    highest = call(
        functools.partial(pairs_kernel, docs),
        shape((slots // LANES, LANES), F32),
        [VMEM, VMEM, VMEM],
        cost=2 * slots * slots * features * mp_size,
    )(arrived.reshape(dp_size, mp_size, capacity, features), key_rows, key_columns)
    sent = jnp.broadcast_to(highest.reshape(dp_size, 1, capacity), (dp_size, mp_size, capacity))
    results = lax.all_to_all(sent.reshape(devices, capacity), ("dp", "mp"), split_axis=0, concat_axis=0, tiled=True)
    picked = call(
        functools.partial(pick_kernel, capacity),
        shape((tiles, LANES), F32),
        [VMEM, VMEM],
        cost=10**8,
    )(results, targets)
    return picked.reshape(block_rows)


def solution(mesh):
    return jax.shard_map(
        shards,
        mesh=mesh,
        in_specs=(P("dp", "mp"), P(), P()),
        out_specs=P("dp"),
        check_vma=False,
    )
```

```python
import functools

import jax
import jax.numpy as jnp
from jax import lax
from jax.experimental import pallas as pl
from jax.experimental.pallas import tpu as pltpu
from jax.sharding import PartitionSpec as P

CL_DEV = 32
LANES = 128
F32, BF16, I32 = jnp.float32, jnp.bfloat16, jnp.int32
VMEM = pl.BlockSpec(memory_space=pltpu.VMEM)
SMEM = pl.BlockSpec(memory_space=pltpu.SMEM)
AXES = ("dp", "mp")


def iota(shape, dimension):
    return lax.broadcasted_iota(I32, shape, dimension)


def dot(a, b):
    return lax.dot_general(a, b, (((1,), (0,)), ((), ())), preferred_element_type=F32)


def dot_nt(a, b):
    return lax.dot_general(a, b, (((1,), (1,)), ((), ())), preferred_element_type=F32)


def column(row):
    return jnp.transpose(jnp.broadcast_to(row, (LANES, LANES)))


def ones_where(mask):
    return jnp.where(mask, 1.0, 0.0)


def to_bf16(mask):
    return ones_where(mask).astype(BF16)


def earlier_lanes():
    return to_bf16(iota((LANES, LANES), 0) < iota((LANES, LANES), 1))


def pair_owners(dp_size, owner_count, cluster_ref):
    block_tiles = cluster_ref.shape[0] // dp_size
    owner_ids = iota((owner_count, LANES), 0)
    block_ids = iota((owner_count, LANES), 1)
    counts = jnp.zeros((owner_count, LANES), F32)
    for block in range(dp_size):
        found = jnp.zeros((owner_count, LANES), F32)
        for tile in range(block * block_tiles, (block + 1) * block_tiles):
            found = found + ones_where(owner_ids == cluster_ref[tile : tile + 1, :] // CL_DEV)
        counts = jnp.where(block_ids == block, jnp.sum(found, axis=1, keepdims=True), counts)
    loads = jnp.sum(counts, axis=1, keepdims=True)
    square = (owner_count, owner_count)
    same = iota(square, 0) == iota(square, 1)
    loads_row = jnp.sum(jnp.where(same, loads, 0.0), axis=0, keepdims=True)
    lighter = (loads_row < loads) | ((loads_row == loads) & (iota(square, 1) < iota(square, 0)))
    return counts, jnp.sum(ones_where(lighter), axis=1, keepdims=True)


def plan_kernel(dp_size, half, place, cluster_ref, target_ref, pair_ref, fits_ref):
    owner_count = pair_ref.shape[0]
    tiles = target_ref.shape[0]
    counts, position = pair_owners(dp_size, owner_count, cluster_ref)
    square = (owner_count, owner_count)
    same = iota(square, 0) == iota(square, 1)
    position_row = jnp.sum(jnp.where(same, position, 0.0), axis=0, keepdims=True)
    partner = position_row == owner_count - 1 - position
    partner_counts = dot(to_bf16(partner), counts.astype(BF16))
    heavier = position >= owner_count // 2
    chip = jnp.where(heavier, owner_count - 1 - position, position)
    fits_ref[0] = (jnp.max(counts + partner_counts) <= 2 * half).astype(I32)
    my_chip = place[1] // 2
    code = jnp.where(chip == my_chip.astype(F32), jnp.where(heavier, 2.0, 1.0), 0.0)
    pair_ref[...] = jnp.broadcast_to(code, pair_ref.shape)
    base = chip * (2 * half) + jnp.where(heavier, partner_counts, 0.0)
    base = jnp.sum(jnp.where(iota(base.shape, 1) == place[0], base, 0.0), axis=1, keepdims=True)
    first = pl.multiple_of(place[0] * tiles, 8)
    earlier = earlier_lanes()
    owner_ids = iota((owner_count, LANES), 0)
    for tile in range(tiles):
        mine = owner_ids == cluster_ref[pl.ds(first + tile, 1), :] // CL_DEV
        counted = dot(to_bf16(mine), earlier) + base
        target_ref[tile : tile + 1, :] = jnp.sum(jnp.where(mine, counted, 0.0), axis=0, keepdims=True).astype(I32)
        base = base + jnp.sum(ones_where(mine), axis=1, keepdims=True)


def pack_kernel(x_ref, sums_ref, target_ref, out_ref, rows, picks):
    tiles = x_ref.shape[0] // LANES
    step = picks.shape[0]
    for tile in range(tiles):
        total = jnp.sum(sums_ref[:, tile, :], axis=0, keepdims=True)
        scale = column(lax.rsqrt(total + 1e-06))
        span = slice(tile * LANES, (tile + 1) * LANES)
        for part in range(x_ref.shape[1] // LANES):
            lanes = slice(part * LANES, (part + 1) * LANES)
            rows[span, lanes] = (x_ref[span, lanes] * scale).astype(BF16)

    slot_ids = iota((LANES, LANES), 0).astype(BF16)

    def fill(index, _):
        for group in range(step // LANES):
            base = (index * (step // LANES) + group) * LANES
            for tile in range(tiles):
                local = target_ref[tile : tile + 1, :] - base
                local = jnp.where((local >= 0) & (local < LANES), local, -1).astype(F32).astype(BF16)
                picks[group * LANES : (group + 1) * LANES, tile * LANES : (tile + 1) * LANES] = jnp.where(
                    slot_ids == local, jnp.ones((), BF16), jnp.zeros((), BF16)
                )
        start = pl.multiple_of(index * step, step)
        out_ref[pl.ds(start, step), :] = dot(picks[...], rows[...]).astype(BF16)
        return 0

    lax.fori_loop(0, out_ref.shape[0] // step, fill, 0)


def keys_kernel(dp_size, half, docs, place, cluster_ref, order_ref, pair_ref, row_ref, column_ref):
    tiles = cluster_ref.shape[0]
    owner_count = pair_ref.shape[0]
    block_tiles = tiles // dp_size
    core = place[1] % 2
    code = pair_ref[:, 0:1]
    ids = iota((owner_count, 1), 0).astype(F32)
    owners = cluster_ref[...] // CL_DEV
    earlier = earlier_lanes()
    tile_row, tile_column = iota((tiles, tiles), 0), iota((tiles, tiles), 1)
    same_block = tile_column // block_tiles == tile_row // block_tiles
    before = to_bf16((tile_column < tile_row) & same_block)
    offset = jnp.zeros((tiles, LANES), F32)
    position = jnp.full((tiles, LANES), -1.0, F32)
    for which in (1.0, 2.0):
        owner = jnp.sum(jnp.where(code == which, ids, 0.0), axis=0, keepdims=True).astype(I32)
        mine = owners == owner
        totals = jnp.sum(ones_where(mine), axis=1, keepdims=True).astype(BF16)
        totals = jnp.broadcast_to(totals, (tiles, LANES))
        rank = dot(to_bf16(mine), earlier) + dot(before, totals) + offset
        position = jnp.where(mine, rank, position)
        offset = dot(to_bf16(same_block), totals)
    position = position.astype(I32)
    in_half = (position >= half).astype(I32)
    lane = jnp.where(position < 0, -1, position - in_half * half + jnp.where(in_half == core, 0, LANES))
    keys = cluster_ref[...] * docs + order_ref[...] + 1
    slot_ids = iota((2 * LANES, LANES), 0)
    for block in range(dp_size):
        total = jnp.zeros((8, 2 * LANES), F32)
        for tile in range(block * block_tiles, (block + 1) * block_tiles):
            key = keys[tile : tile + 1, :]
            pieces = [((key >> (8 * piece)) & 255).astype(F32) for piece in range(4)]
            pieces = jnp.concatenate(pieces + [jnp.zeros((4, LANES), F32)], axis=0).astype(BF16)
            total = total + dot_nt(pieces, to_bf16(slot_ids == lane[tile : tile + 1, :]))
        total = total.astype(I32)
        key = total[0:1] + (total[1:2] << 8) + (total[2:3] << 16) + (total[3:4] << 24) - 1
        for side in range(2):
            start = (side * dp_size + block) * half
            column_ref[start : start + half, :] = column(key[:, side * LANES : (side + 1) * LANES])[:half]
    for group in range(row_ref.shape[0]):
        row_ref[group : group + 1, :] = jnp.transpose(column_ref[group * LANES : (group + 1) * LANES, :])[0:1]


def pairs_kernel(docs, own_ref, early_ref, row_ref, column_ref, best_ref, out_ref):
    dp_size, mp_size, half, features = own_ref.shape
    slots = dp_size * half

    def whole(ref):
        parts = [ref[:, part].reshape(slots, features) for part in range(mp_size)]
        return jnp.concatenate(parts, axis=1)

    early = whole(early_ref)
    own = early if own_ref is early_ref else whole(own_ref)
    start = 0
    while start < slots:
        width = min(2 * LANES, slots - start)
        groups = range(start // LANES, (start + width) // LANES)
        key = jnp.concatenate([row_ref[group : group + 1, :] for group in groups], axis=1)
        lowest = jnp.where(key < 0, 0, (key // docs) * docs)
        cosines = dot_nt(early, own[start : start + width])
        keys = jnp.concatenate([column_ref[...]] * len(groups), axis=1)
        good = (keys >= lowest) & (keys < key)
        best = jnp.max(jnp.where(good, cosines, 0.0), axis=0, keepdims=True)
        for group in groups:
            lanes = slice(group * LANES - start, (group + 1) * LANES - start)
            found = best[:, lanes]
            if best_ref is not None:
                found = jnp.maximum(found, best_ref[group : group + 1, :])
            out_ref[group : group + 1, :] = found
        start += width


def own_pairs_kernel(docs, own_ref, row_ref, column_ref, out_ref):
    pairs_kernel(docs, own_ref, own_ref, row_ref, column_ref, None, out_ref)


def pick_kernel(results_ref, target_ref, out_ref):
    device_count, half = results_ref.shape
    tiles = target_ref.shape[0]
    results = results_ref[...]
    high = results.astype(BF16)
    rest = results - high.astype(F32)
    middle = rest.astype(BF16)
    low = (rest - middle.astype(F32)).astype(BF16)
    pieces = jnp.concatenate([high, middle, low], axis=0)
    device_ids = iota((device_count, LANES), 0)
    rank_ids = iota((half, LANES), 0)
    for tile in range(tiles):
        target = target_ref[tile : tile + 1, :]
        device = target // half
        one_hot = to_bf16(device_ids == device)
        one_hot = jnp.concatenate([one_hot, one_hot, one_hot], axis=0)
        ranked = lax.dot_general(pieces, one_hot, (((0,), (0,)), ((), ())), preferred_element_type=F32)
        hit = rank_ids == target - device * half
        out_ref[tile : tile + 1, :] = jnp.sum(jnp.where(hit, ranked, 0.0), axis=0, keepdims=True)


def call(kernel, out_shape, specs, out_specs=None, scratch=(), cost=0, megabytes=32):
    return pl.pallas_call(
        kernel,
        out_shape=out_shape,
        in_specs=specs,
        out_specs=out_specs or jax.tree.map(lambda _: VMEM, out_shape),
        scratch_shapes=list(scratch),
        compiler_params=pltpu.CompilerParams(vmem_limit_bytes=megabytes << 20),
        cost_estimate=pl.CostEstimate(flops=cost, bytes_accessed=1 << 20, transcendentals=0),
    )


def routed(half, place, embeddings, sums, clusters, orders):
    shape = jax.ShapeDtypeStruct
    block_rows, features = embeddings.shape
    docs = clusters.shape[0] * LANES
    dp_size, mp_size = lax.axis_size("dp"), lax.axis_size("mp")
    devices = dp_size * mp_size
    tiles = block_rows // LANES
    slots = dp_size * half
    targets, pair, fits = call(
        functools.partial(plan_kernel, dp_size, half),
        (shape((tiles, LANES), I32), shape((devices, LANES), F32), shape((1,), I32)),
        [SMEM, VMEM],
        (VMEM, VMEM, SMEM),
        cost=10**8,
    )(place, clusters)
    step = 512 if devices * half % 512 == 0 else LANES
    outgoing = call(
        pack_kernel,
        shape((devices * half, features), BF16),
        [VMEM, VMEM, VMEM],
        None,
        [pltpu.VMEM((block_rows, features), BF16), pltpu.VMEM((step, block_rows), BF16)],
        2 * devices * half * block_rows * features,
    )(embeddings, sums, targets)
    arrived = lax.all_to_all(
        outgoing.reshape(devices, half, features), AXES, split_axis=0, concat_axis=0, tiled=True
    ).reshape(dp_size, mp_size, half, features)
    key_rows, key_columns = call(
        functools.partial(keys_kernel, dp_size, half, docs),
        (shape((slots // LANES, LANES), I32), shape((2 * slots, LANES), I32)),
        [SMEM, VMEM, VMEM, VMEM],
        cost=10**9,
    )(place, clusters, orders, pair)
    other = lax.ppermute(arrived, "mp", [(i, i ^ 1) for i in range(mp_size)])
    work = 2 * slots * slots * features * mp_size
    result = shape((slots // LANES, LANES), F32)
    best = call(functools.partial(own_pairs_kernel, docs), result, [VMEM] * 3, cost=work)(
        arrived, key_rows, key_columns[:slots]
    )
    highest = call(functools.partial(pairs_kernel, docs), result, [VMEM] * 5, cost=work)(
        arrived, other, key_rows, key_columns[slots:], best
    )
    sent = jnp.broadcast_to(highest.reshape(dp_size, 1, half), (dp_size, mp_size, half))
    results = lax.all_to_all(sent.reshape(devices, half), AXES, split_axis=0, concat_axis=0, tiled=True)
    picked = call(pick_kernel, shape((tiles, LANES), F32), [VMEM, VMEM], cost=10**8)(results, targets)
    return picked.reshape(block_rows), fits[0]


def shards(embeddings, cluster_of, doc_order):
    block_rows, _ = embeddings.shape
    docs = cluster_of.shape[0]
    mp_size = lax.axis_size("mp")
    devices = lax.axis_size("dp") * mp_size
    most = 2 * block_rows // devices
    half = -(-5 * most // 8 // 16) * 16
    dp_index, mp_index = lax.axis_index("dp"), lax.axis_index("mp")
    place = jnp.stack([dp_index, dp_index * mp_size + mp_index]).astype(I32)
    clusters = cluster_of.reshape(docs // LANES, LANES)
    orders = doc_order.reshape(docs // LANES, LANES)
    squares = jnp.sum(embeddings * embeddings, axis=1).reshape(block_rows // LANES, LANES)
    sums = lax.all_gather(squares, "mp")
    arrays = (place, embeddings, sums, clusters, orders)
    picked, fits = routed(half, *arrays)
    if half == most:
        return picked
    return lax.cond(fits == 1, lambda *_: picked, lambda *rest: routed(most, *rest)[0], *arrays)


def solution(mesh):
    return jax.shard_map(
        shards,
        mesh=mesh,
        in_specs=(P("dp", "mp"), P(), P()),
        out_specs=P("dp"),
        check_vma=False,
    )
```

```python
import functools

import jax
import jax.numpy as jnp
from jax import lax
from jax.experimental import pallas as pl
from jax.experimental.pallas import tpu as pltpu
from jax.sharding import PartitionSpec as P

CL_DEV = 32
LANES = 128
F32, BF16, I32 = jnp.float32, jnp.bfloat16, jnp.int32
VMEM = pl.BlockSpec(memory_space=pltpu.VMEM)
SMEM = pl.BlockSpec(memory_space=pltpu.SMEM)
AXES = ("dp", "mp")


def iota(shape, dimension):
    return lax.broadcasted_iota(I32, shape, dimension)


def dot(a, b):
    return lax.dot_general(a, b, (((1,), (0,)), ((), ())), preferred_element_type=F32)


def dot_nt(a, b):
    return lax.dot_general(a, b, (((1,), (1,)), ((), ())), preferred_element_type=F32)


def column(row):
    return jnp.transpose(jnp.broadcast_to(row, (LANES, LANES)))


def ones_where(mask):
    return jnp.where(mask, 1.0, 0.0)


def to_bf16(mask):
    return ones_where(mask).astype(BF16)


def earlier_lanes():
    return to_bf16(iota((LANES, LANES), 0) < iota((LANES, LANES), 1))


def pair_owners(dp_size, owner_count, cluster_ref):
    block_tiles = cluster_ref.shape[0] // dp_size
    owner_ids = iota((owner_count, LANES), 0)
    block_ids = iota((owner_count, LANES), 1)
    counts = jnp.zeros((owner_count, LANES), F32)
    for block in range(dp_size):
        found = jnp.zeros((owner_count, LANES), F32)
        for tile in range(block * block_tiles, (block + 1) * block_tiles):
            found = found + ones_where(owner_ids == cluster_ref[tile : tile + 1, :] // CL_DEV)
        counts = jnp.where(block_ids == block, jnp.sum(found, axis=1, keepdims=True), counts)
    loads = jnp.sum(counts, axis=1, keepdims=True)
    square = (owner_count, owner_count)
    same = iota(square, 0) == iota(square, 1)
    loads_row = jnp.sum(jnp.where(same, loads, 0.0), axis=0, keepdims=True)
    lighter = (loads_row < loads) | ((loads_row == loads) & (iota(square, 1) < iota(square, 0)))
    return counts, jnp.sum(ones_where(lighter), axis=1, keepdims=True)


def plan_kernel(dp_size, half, place, cluster_ref, target_ref, pair_ref, fits_ref):
    owner_count = pair_ref.shape[0]
    tiles = target_ref.shape[0]
    counts, position = pair_owners(dp_size, owner_count, cluster_ref)
    square = (owner_count, owner_count)
    same = iota(square, 0) == iota(square, 1)
    position_row = jnp.sum(jnp.where(same, position, 0.0), axis=0, keepdims=True)
    partner = position_row == owner_count - 1 - position
    partner_counts = dot(to_bf16(partner), counts.astype(BF16))
    heavier = position >= owner_count // 2
    chip = jnp.where(heavier, owner_count - 1 - position, position)
    fits_ref[0] = (jnp.max(counts + partner_counts) <= 2 * half).astype(I32)
    my_chip = place[1] // 2
    code = jnp.where(chip == my_chip.astype(F32), jnp.where(heavier, 2.0, 1.0), 0.0)
    pair_ref[...] = jnp.broadcast_to(code, pair_ref.shape)
    base = chip * (2 * half) + jnp.where(heavier, partner_counts, 0.0)
    base = jnp.sum(jnp.where(iota(base.shape, 1) == place[0], base, 0.0), axis=1, keepdims=True)
    first = pl.multiple_of(place[0] * tiles, 8)
    earlier = earlier_lanes()
    owner_ids = iota((owner_count, LANES), 0)
    for tile in range(tiles):
        mine = owner_ids == cluster_ref[pl.ds(first + tile, 1), :] // CL_DEV
        counted = dot(to_bf16(mine), earlier) + base
        target_ref[tile : tile + 1, :] = jnp.sum(jnp.where(mine, counted, 0.0), axis=0, keepdims=True).astype(I32)
        base = base + jnp.sum(ones_where(mine), axis=1, keepdims=True)


def pack_kernel(x_ref, target_ref, *refs):
    *sum_refs, out_ref, rows, picks = refs
    tiles = x_ref.shape[0] // LANES
    step = picks.shape[0]
    for tile in range(tiles):
        total = sum(ref[tile : tile + 1, :] for ref in sum_refs)
        scale = column(lax.rsqrt(total + 1e-06))
        span = slice(tile * LANES, (tile + 1) * LANES)
        for part in range(x_ref.shape[1] // LANES):
            lanes = slice(part * LANES, (part + 1) * LANES)
            rows[span, lanes] = (x_ref[span, lanes] * scale).astype(BF16)

    slot_ids = iota((LANES, LANES), 0).astype(BF16)

    def fill(index, _):
        for group in range(step // LANES):
            base = (index * (step // LANES) + group) * LANES
            for tile in range(tiles):
                local = target_ref[tile : tile + 1, :] - base
                local = jnp.where((local >= 0) & (local < LANES), local, -1).astype(F32).astype(BF16)
                picks[group * LANES : (group + 1) * LANES, tile * LANES : (tile + 1) * LANES] = jnp.where(
                    slot_ids == local, jnp.ones((), BF16), jnp.zeros((), BF16)
                )
        start = pl.multiple_of(index * step, step)
        out_ref[pl.ds(start, step), :] = dot(picks[...], rows[...]).astype(BF16)
        return 0

    lax.fori_loop(0, out_ref.shape[0] // step, fill, 0)


def keys_kernel(dp_size, half, docs, place, cluster_ref, order_ref, pair_ref, row_ref, own_ref, other_ref):
    tiles = cluster_ref.shape[0]
    owner_count = pair_ref.shape[0]
    block_tiles = tiles // dp_size
    core = place[1] % 2
    code = pair_ref[:, 0:1]
    ids = iota((owner_count, 1), 0).astype(F32)
    owners = cluster_ref[...] // CL_DEV
    earlier = earlier_lanes()
    tile_row, tile_column = iota((tiles, tiles), 0), iota((tiles, tiles), 1)
    same_block = tile_column // block_tiles == tile_row // block_tiles
    before = to_bf16((tile_column < tile_row) & same_block)
    offset = jnp.zeros((tiles, LANES), F32)
    position = jnp.full((tiles, LANES), -1.0, F32)
    for which in (1.0, 2.0):
        owner = jnp.sum(jnp.where(code == which, ids, 0.0), axis=0, keepdims=True).astype(I32)
        mine = owners == owner
        totals = jnp.sum(ones_where(mine), axis=1, keepdims=True).astype(BF16)
        totals = jnp.broadcast_to(totals, (tiles, LANES))
        rank = dot(to_bf16(mine), earlier) + dot(before, totals) + offset
        position = jnp.where(mine, rank, position)
        offset = dot(to_bf16(same_block), totals)
    position = position.astype(I32)
    in_half = (position >= half).astype(I32)
    lane = jnp.where(position < 0, -1, position - in_half * half + jnp.where(in_half == core, 0, LANES))
    keys = cluster_ref[...] * docs + order_ref[...] + 1
    slot_ids = iota((2 * LANES, LANES), 0)
    for block in range(dp_size):
        total = jnp.zeros((8, 2 * LANES), F32)
        for tile in range(block * block_tiles, (block + 1) * block_tiles):
            key = keys[tile : tile + 1, :]
            pieces = [((key >> (8 * piece)) & 255).astype(F32) for piece in range(4)]
            pieces = jnp.concatenate(pieces + [jnp.zeros((4, LANES), F32)], axis=0).astype(BF16)
            total = total + dot_nt(pieces, to_bf16(slot_ids == lane[tile : tile + 1, :]))
        total = total.astype(I32)
        key = total[0:1] + (total[1:2] << 8) + (total[2:3] << 16) + (total[3:4] << 24) - 1
        for side, ref in enumerate((own_ref, other_ref)):
            ref[block * half : (block + 1) * half, :] = column(key[:, side * LANES : (side + 1) * LANES])[:half]
    for group in range(row_ref.shape[0]):
        row_ref[group : group + 1, :] = jnp.transpose(own_ref[group * LANES : (group + 1) * LANES, :])[0:1]


def pairs_kernel(docs, own_ref, early_ref, row_ref, column_ref, best_ref, out_ref):
    dp_size, mp_size, half, features = own_ref.shape
    slots = dp_size * half

    def whole(ref):
        parts = [ref[:, part].reshape(slots, features) for part in range(mp_size)]
        return jnp.concatenate(parts, axis=1)

    early = whole(early_ref)
    own = early if own_ref is early_ref else whole(own_ref)
    start, found = 0, []
    while start < slots:
        width = min(2 * LANES, slots - start)
        groups = range(start // LANES, (start + width) // LANES)
        key = jnp.concatenate([row_ref[group : group + 1, :] for group in groups], axis=1)
        lowest = jnp.where(key < 0, 0, (key // docs) * docs)
        cosines = dot_nt(early, own[start : start + width])
        keys = jnp.concatenate([column_ref[...]] * len(groups), axis=1)
        good = (keys >= lowest) & (keys < key)
        found.append(jnp.max(jnp.where(good, cosines, 0.0), axis=0, keepdims=True))
        start += width
    found = jnp.concatenate(found, axis=1)
    if best_ref is None:
        out_ref[...] = found
        return
    found = jnp.maximum(found, best_ref[...])
    for block in range(dp_size):
        out_ref[block] = jnp.broadcast_to(found[:, block * half : (block + 1) * half], (mp_size, half))


def own_pairs_kernel(docs, own_ref, row_ref, column_ref, out_ref):
    pairs_kernel(docs, own_ref, own_ref, row_ref, column_ref, None, out_ref)


def pick_kernel(results_ref, target_ref, out_ref):
    device_count, half = results_ref.shape
    tiles = target_ref.shape[0]
    results = results_ref[...]
    high = results.astype(BF16)
    rest = results - high.astype(F32)
    middle = rest.astype(BF16)
    low = (rest - middle.astype(F32)).astype(BF16)
    pieces = jnp.concatenate([high, middle, low], axis=0)
    device_ids = iota((device_count, LANES), 0)
    rank_ids = iota((half, LANES), 0)
    for tile in range(tiles):
        target = target_ref[tile : tile + 1, :]
        device = target // half
        one_hot = to_bf16(device_ids == device)
        one_hot = jnp.concatenate([one_hot, one_hot, one_hot], axis=0)
        ranked = lax.dot_general(pieces, one_hot, (((0,), (0,)), ((), ())), preferred_element_type=F32)
        hit = rank_ids == target - device * half
        out_ref[tile : tile + 1, :] = jnp.sum(jnp.where(hit, ranked, 0.0), axis=0, keepdims=True)


def call(kernel, out_shape, specs, out_specs=None, scratch=(), cost=0, megabytes=32):
    return pl.pallas_call(
        kernel,
        out_shape=out_shape,
        in_specs=specs,
        out_specs=out_specs or jax.tree.map(lambda _: VMEM, out_shape),
        scratch_shapes=list(scratch),
        compiler_params=pltpu.CompilerParams(vmem_limit_bytes=megabytes << 20),
        cost_estimate=pl.CostEstimate(flops=cost, bytes_accessed=1 << 20, transcendentals=0),
    )


def routed(half, place, embeddings, sums, clusters, orders):
    shape = jax.ShapeDtypeStruct
    block_rows, features = embeddings.shape
    docs = clusters.shape[0] * LANES
    dp_size, mp_size = lax.axis_size("dp"), lax.axis_size("mp")
    devices = dp_size * mp_size
    tiles = block_rows // LANES
    slots = dp_size * half
    targets, pair, fits = call(
        functools.partial(plan_kernel, dp_size, half),
        (shape((tiles, LANES), I32), shape((devices, LANES), F32), shape((1,), I32)),
        [SMEM, VMEM],
        (VMEM, VMEM, SMEM),
        cost=10**8,
    )(place, clusters)
    step = 512 if devices * half % 512 == 0 else LANES
    outgoing = call(
        pack_kernel,
        shape((devices * half, features), BF16),
        [VMEM] * (2 + mp_size),
        None,
        [pltpu.VMEM((block_rows, features), BF16), pltpu.VMEM((step, block_rows), BF16)],
        2 * devices * half * block_rows * features,
    )(embeddings, targets, *sums)
    sources, outgoing = lax.optimization_barrier(((clusters, orders, pair), outgoing))
    arrived = lax.all_to_all(
        outgoing.reshape(devices, half, features), AXES, split_axis=0, concat_axis=0, tiled=True
    ).reshape(dp_size, mp_size, half, features)
    key_rows, own_columns, other_columns = call(
        functools.partial(keys_kernel, dp_size, half, docs),
        (shape((slots // LANES, LANES), I32), *[shape((slots, LANES), I32)] * 2),
        [SMEM, VMEM, VMEM, VMEM],
        cost=10**9,
    )(place, *sources)
    arrived, key_rows = lax.optimization_barrier((arrived, key_rows))
    other = lax.ppermute(arrived, "mp", [(i, i ^ 1) for i in range(mp_size)])
    work = 2 * slots * slots * features * mp_size
    best = call(functools.partial(own_pairs_kernel, docs), shape((1, slots), F32), [VMEM] * 3, cost=work)(
        arrived, key_rows, own_columns
    )
    highest = call(
        functools.partial(pairs_kernel, docs), shape((dp_size, mp_size, half), F32), [VMEM] * 5, cost=work
    )(arrived, other, key_rows, other_columns, best)
    results = lax.all_to_all(
        highest.reshape(devices, half), AXES, split_axis=0, concat_axis=0, tiled=True
    )
    return results, targets, fits[0]


def pick(results, targets):
    picked = call(
        pick_kernel, jax.ShapeDtypeStruct(targets.shape, F32), [VMEM, VMEM], cost=10**8
    )(results, targets)
    return picked.reshape(targets.size)


def shards(embeddings, cluster_of, doc_order):
    block_rows, _ = embeddings.shape
    docs = cluster_of.shape[0]
    mp_size = lax.axis_size("mp")
    devices = lax.axis_size("dp") * mp_size
    most = 2 * block_rows // devices
    half = -(-5 * most // 8 // 16) * 16
    dp_index, mp_index = lax.axis_index("dp"), lax.axis_index("mp")
    place = jnp.stack([dp_index, dp_index * mp_size + mp_index]).astype(I32)
    clusters = cluster_of.reshape(docs // LANES, LANES)
    orders = doc_order.reshape(docs // LANES, LANES)
    squares = jnp.sum(embeddings * embeddings, axis=1).reshape(block_rows // LANES, LANES)
    others = [lax.ppermute(squares, "mp", [(i, i ^ k) for i in range(mp_size)]) for k in range(mp_size - 1, 0, -1)]
    sums = (squares, *others)
    arrays = (place, embeddings, sums, clusters, orders)
    results, targets, fits = routed(half, *arrays)
    if half == most:
        return pick(results, targets)
    return lax.cond(
        fits == 1,
        lambda results, targets, *_: pick(results, targets),
        lambda _results, _targets, *rest: pick(*routed(most, *rest)[:2]),
        results,
        targets,
        *arrays,
    )


def solution(mesh):
    return jax.shard_map(
        shards,
        mesh=mesh,
        in_specs=(P("dp", "mp"), P(), P()),
        out_specs=P("dp"),
        check_vma=False,
    )
```

```python
import functools

import jax
import jax.numpy as jnp
from jax import lax
from jax.experimental import pallas as pl
from jax.experimental.pallas import tpu as pltpu
from jax.sharding import PartitionSpec as P

CL_DEV = 32
LANES = 128
F32, BF16, I32 = jnp.float32, jnp.bfloat16, jnp.int32
VMEM = pl.BlockSpec(memory_space=pltpu.VMEM)
SMEM = pl.BlockSpec(memory_space=pltpu.SMEM)
AXES = ("dp", "mp")


def iota(shape, dimension):
    return lax.broadcasted_iota(I32, shape, dimension)


def dot(a, b):
    return lax.dot_general(a, b, (((1,), (0,)), ((), ())), preferred_element_type=F32)


def dot_nt(a, b):
    return lax.dot_general(a, b, (((1,), (1,)), ((), ())), preferred_element_type=F32)


def column(row):
    return jnp.transpose(jnp.broadcast_to(row, (LANES, LANES)))


def ones_where(mask):
    return jnp.where(mask, 1.0, 0.0)


def to_bf16(mask):
    return ones_where(mask).astype(BF16)


def earlier_lanes():
    return to_bf16(iota((LANES, LANES), 0) < iota((LANES, LANES), 1))


def pair_owners(dp_size, owner_count, cluster_ref):
    block_tiles = cluster_ref.shape[0] // dp_size
    owner_ids = iota((owner_count, LANES), 0)
    block_ids = iota((owner_count, LANES), 1)
    counts = jnp.zeros((owner_count, LANES), F32)
    for block in range(dp_size):
        found = jnp.zeros((owner_count, LANES), F32)
        for tile in range(block * block_tiles, (block + 1) * block_tiles):
            found = found + ones_where(owner_ids == cluster_ref[tile : tile + 1, :] // CL_DEV)
        counts = jnp.where(block_ids == block, jnp.sum(found, axis=1, keepdims=True), counts)
    loads = jnp.sum(counts, axis=1, keepdims=True)
    square = (owner_count, owner_count)
    same = iota(square, 0) == iota(square, 1)
    loads_row = jnp.sum(jnp.where(same, loads, 0.0), axis=0, keepdims=True)
    lighter = (loads_row < loads) | ((loads_row == loads) & (iota(square, 1) < iota(square, 0)))
    return counts, jnp.sum(ones_where(lighter), axis=1, keepdims=True)


def plan_kernel(dp_size, half, place, cluster_ref, target_ref, pair_ref, fits_ref):
    owner_count = pair_ref.shape[0]
    tiles = target_ref.shape[0]
    counts, position = pair_owners(dp_size, owner_count, cluster_ref)
    square = (owner_count, owner_count)
    same = iota(square, 0) == iota(square, 1)
    position_row = jnp.sum(jnp.where(same, position, 0.0), axis=0, keepdims=True)
    partner = position_row == owner_count - 1 - position
    partner_counts = dot(to_bf16(partner), counts.astype(BF16))
    heavier = position >= owner_count // 2
    chip = jnp.where(heavier, owner_count - 1 - position, position)
    fits_ref[0] = (jnp.max(counts + partner_counts) <= 2 * half).astype(I32)
    my_chip = place[1] // 2
    code = jnp.where(chip == my_chip.astype(F32), jnp.where(heavier, 2.0, 1.0), 0.0)
    pair_ref[...] = jnp.broadcast_to(code, pair_ref.shape)
    base = chip * (2 * half) + jnp.where(heavier, partner_counts, 0.0)
    base = jnp.sum(jnp.where(iota(base.shape, 1) == place[0], base, 0.0), axis=1, keepdims=True)
    first = pl.multiple_of(place[0] * tiles, 8)
    earlier = earlier_lanes()
    owner_ids = iota((owner_count, LANES), 0)
    for tile in range(tiles):
        mine = owner_ids == cluster_ref[pl.ds(first + tile, 1), :] // CL_DEV
        counted = dot(to_bf16(mine), earlier) + base
        target_ref[tile : tile + 1, :] = jnp.sum(jnp.where(mine, counted, 0.0), axis=0, keepdims=True).astype(I32)
        base = base + jnp.sum(ones_where(mine), axis=1, keepdims=True)


def pack_kernel(x_ref, target_ref, *refs):
    *sum_refs, out_ref, rows, picks = refs
    tiles = x_ref.shape[0] // LANES
    size = out_ref.shape[0]

    @pl.when(pl.program_id(0) == 0)
    def scale_rows():
        for tile in range(tiles):
            total = sum(ref[tile : tile + 1, :] for ref in sum_refs)
            scale = column(lax.rsqrt(total + 1e-06))
            span = slice(tile * LANES, (tile + 1) * LANES)
            for part in range(x_ref.shape[1] // LANES):
                lanes = slice(part * LANES, (part + 1) * LANES)
                rows[span, lanes] = (x_ref[span, lanes] * scale).astype(BF16)

    slot_ids = iota((LANES, LANES), 0).astype(BF16)
    for start in range(0, size, LANES):
        local = target_ref[...] - (pl.program_id(0) * size + start)
        local = jnp.where((local >= 0) & (local < LANES), local, -1).astype(F32)
        for tile in range(tiles):
            hit = slot_ids == local[tile : tile + 1, :].astype(BF16)
            picks[start : start + LANES, tile * LANES : (tile + 1) * LANES] = jnp.where(
                hit, jnp.ones((), BF16), jnp.zeros((), BF16)
            )
    out_ref[...] = dot(picks[...], rows[...]).astype(BF16)


def keys_kernel(dp_size, half, docs, place, cluster_ref, order_ref, pair_ref, row_ref, own_ref, other_ref):
    tiles = cluster_ref.shape[0]
    owner_count = pair_ref.shape[0]
    block_tiles = tiles // dp_size
    core = place[1] % 2
    code = pair_ref[:, 0:1]
    ids = iota((owner_count, 1), 0).astype(F32)
    owners = cluster_ref[...] // CL_DEV
    earlier = earlier_lanes()
    tile_row, tile_column = iota((tiles, tiles), 0), iota((tiles, tiles), 1)
    same_block = tile_column // block_tiles == tile_row // block_tiles
    before = to_bf16((tile_column < tile_row) & same_block)
    offset = jnp.zeros((tiles, LANES), F32)
    position = jnp.full((tiles, LANES), -1.0, F32)
    for which in (1.0, 2.0):
        owner = jnp.sum(jnp.where(code == which, ids, 0.0), axis=0, keepdims=True).astype(I32)
        mine = owners == owner
        totals = jnp.sum(ones_where(mine), axis=1, keepdims=True).astype(BF16)
        totals = jnp.broadcast_to(totals, (tiles, LANES))
        rank = dot(to_bf16(mine), earlier) + dot(before, totals) + offset
        position = jnp.where(mine, rank, position)
        offset = dot(to_bf16(same_block), totals)
    position = position.astype(I32)
    in_half = (position >= half).astype(I32)
    lane = jnp.where(position < 0, -1, position - in_half * half + jnp.where(in_half == core, 0, LANES))
    keys = cluster_ref[...] * docs + order_ref[...] + 1
    slot_ids = iota((2 * LANES, LANES), 0)
    for block in range(dp_size):
        total = jnp.zeros((8, 2 * LANES), F32)
        for tile in range(block * block_tiles, (block + 1) * block_tiles):
            key = keys[tile : tile + 1, :]
            pieces = [((key >> (8 * piece)) & 255).astype(F32) for piece in range(4)]
            pieces = jnp.concatenate(pieces + [jnp.zeros((4, LANES), F32)], axis=0).astype(BF16)
            total = total + dot_nt(pieces, to_bf16(slot_ids == lane[tile : tile + 1, :]))
        total = total.astype(I32)
        key = total[0:1] + (total[1:2] << 8) + (total[2:3] << 16) + (total[3:4] << 24) - 1
        for side, ref in enumerate((own_ref, other_ref)):
            ref[block * half : (block + 1) * half, :] = column(key[:, side * LANES : (side + 1) * LANES])[:half]
    for group in range(row_ref.shape[0]):
        row_ref[group : group + 1, :] = jnp.transpose(own_ref[group * LANES : (group + 1) * LANES, :])[0:1]


def pairs_kernel(docs, own_ref, early_ref, row_ref, column_ref, best_ref, out_ref):
    dp_size, mp_size, half, features = own_ref.shape
    slots = dp_size * half

    def whole(ref):
        parts = [ref[:, part].reshape(slots, features) for part in range(mp_size)]
        return jnp.concatenate(parts, axis=1)

    early = whole(early_ref)
    own = early if own_ref is early_ref else whole(own_ref)
    start, found = 0, []
    while start < slots:
        width = min(2 * LANES, slots - start)
        groups = range(start // LANES, (start + width) // LANES)
        key = jnp.concatenate([row_ref[group : group + 1, :] for group in groups], axis=1)
        lowest = jnp.where(key < 0, 0, (key // docs) * docs)
        cosines = dot_nt(early, own[start : start + width])
        keys = jnp.concatenate([column_ref[...]] * len(groups), axis=1)
        good = (keys >= lowest) & (keys < key)
        found.append(jnp.max(jnp.where(good, cosines, 0.0), axis=0, keepdims=True))
        start += width
    found = jnp.concatenate(found, axis=1)
    if best_ref is None:
        out_ref[...] = found
        return
    found = jnp.maximum(found, best_ref[...])
    for block in range(dp_size):
        out_ref[block] = jnp.broadcast_to(found[:, block * half : (block + 1) * half], (mp_size, half))


def own_pairs_kernel(docs, own_ref, row_ref, column_ref, out_ref):
    pairs_kernel(docs, own_ref, own_ref, row_ref, column_ref, None, out_ref)


def pick_kernel(results_ref, target_ref, out_ref):
    device_count, half = results_ref.shape
    tiles = target_ref.shape[0]
    results = results_ref[...]
    high = results.astype(BF16)
    rest = results - high.astype(F32)
    middle = rest.astype(BF16)
    low = (rest - middle.astype(F32)).astype(BF16)
    pieces = jnp.concatenate([high, middle, low], axis=0)
    device_ids = iota((device_count, LANES), 0)
    rank_ids = iota((half, LANES), 0)
    for tile in range(tiles):
        target = target_ref[tile : tile + 1, :]
        device = target // half
        one_hot = to_bf16(device_ids == device)
        one_hot = jnp.concatenate([one_hot, one_hot, one_hot], axis=0)
        ranked = lax.dot_general(pieces, one_hot, (((0,), (0,)), ((), ())), preferred_element_type=F32)
        hit = rank_ids == target - device * half
        out_ref[tile : tile + 1, :] = jnp.sum(jnp.where(hit, ranked, 0.0), axis=0, keepdims=True)


def call(kernel, out_shape, specs, out_specs=None, scratch=(), cost=0, megabytes=32):
    return pl.pallas_call(
        kernel,
        out_shape=out_shape,
        in_specs=specs,
        out_specs=out_specs or jax.tree.map(lambda _: VMEM, out_shape),
        scratch_shapes=list(scratch),
        compiler_params=pltpu.CompilerParams(vmem_limit_bytes=megabytes << 20),
        cost_estimate=pl.CostEstimate(flops=cost, bytes_accessed=1 << 20, transcendentals=0),
    )


def routed(half, place, embeddings, sums, clusters, orders):
    shape = jax.ShapeDtypeStruct
    block_rows, features = embeddings.shape
    docs = clusters.shape[0] * LANES
    dp_size, mp_size = lax.axis_size("dp"), lax.axis_size("mp")
    devices = dp_size * mp_size
    tiles = block_rows // LANES
    slots = dp_size * half
    targets, pair, fits = call(
        functools.partial(plan_kernel, dp_size, half),
        (shape((tiles, LANES), I32), shape((devices, LANES), F32), shape((1,), I32)),
        [SMEM, VMEM],
        (VMEM, VMEM, SMEM),
        cost=10**8,
    )(place, clusters)
    size = max(size for size in range(LANES, 1281, LANES) if devices * half % size == 0)

    def whole(array):
        return pl.BlockSpec(array.shape, lambda step: (0, 0))

    packed = (embeddings, targets, *sums)
    outgoing = pl.pallas_call(
        pack_kernel,
        grid=(devices * half // size,),
        out_shape=shape((devices * half, features), BF16),
        in_specs=[whole(array) for array in packed],
        out_specs=pl.BlockSpec((size, features), lambda step: (step, 0)),
        scratch_shapes=[pltpu.VMEM((block_rows, features), BF16), pltpu.VMEM((size, block_rows), BF16)],
        compiler_params=pltpu.CompilerParams(vmem_limit_bytes=40 << 20),
    )(*packed)
    sources, outgoing = lax.optimization_barrier(((clusters, orders, pair), outgoing))
    arrived = lax.all_to_all(
        outgoing.reshape(devices, half, features), AXES, split_axis=0, concat_axis=0, tiled=True
    ).reshape(dp_size, mp_size, half, features)
    key_rows, own_columns, other_columns = call(
        functools.partial(keys_kernel, dp_size, half, docs),
        (shape((slots // LANES, LANES), I32), *[shape((slots, LANES), I32)] * 2),
        [SMEM, VMEM, VMEM, VMEM],
        cost=10**9,
    )(place, *sources)
    arrived, key_rows = lax.optimization_barrier((arrived, key_rows))
    other = lax.ppermute(arrived, "mp", [(i, i ^ 1) for i in range(mp_size)])
    work = 2 * slots * slots * features * mp_size
    best = call(functools.partial(own_pairs_kernel, docs), shape((1, slots), F32), [VMEM] * 3, cost=work)(
        arrived, key_rows, own_columns
    )
    highest = call(
        functools.partial(pairs_kernel, docs), shape((dp_size, mp_size, half), F32), [VMEM] * 5, cost=work
    )(arrived, other, key_rows, other_columns, best)
    results = lax.all_to_all(
        highest.reshape(devices, half), AXES, split_axis=0, concat_axis=0, tiled=True
    )
    return results, targets, fits[0]


def pick(results, targets):
    picked = call(
        pick_kernel, jax.ShapeDtypeStruct(targets.shape, F32), [VMEM, VMEM], cost=10**8
    )(results, targets)
    return picked.reshape(targets.size)


def shards(embeddings, cluster_of, doc_order):
    block_rows, _ = embeddings.shape
    docs = cluster_of.shape[0]
    mp_size = lax.axis_size("mp")
    devices = lax.axis_size("dp") * mp_size
    most = 2 * block_rows // devices
    half = -(-5 * most // 8 // 16) * 16
    dp_index, mp_index = lax.axis_index("dp"), lax.axis_index("mp")
    place = jnp.stack([dp_index, dp_index * mp_size + mp_index]).astype(I32)
    clusters = cluster_of.reshape(docs // LANES, LANES)
    orders = doc_order.reshape(docs // LANES, LANES)
    squares = jnp.sum(embeddings * embeddings, axis=1).reshape(block_rows // LANES, LANES)
    others = [lax.ppermute(squares, "mp", [(i, i ^ k) for i in range(mp_size)]) for k in range(mp_size - 1, 0, -1)]
    sums = (squares, *others)
    arrays = (place, embeddings, sums, clusters, orders)
    results, targets, fits = routed(half, *arrays)
    if half == most:
        return pick(results, targets)
    return lax.cond(
        fits == 1,
        lambda results, targets, *_: pick(results, targets),
        lambda _results, _targets, *rest: pick(*routed(most, *rest)[:2]),
        results,
        targets,
        *arrays,
    )


def solution(mesh):
    return jax.shard_map(
        shards,
        mesh=mesh,
        in_specs=(P("dp", "mp"), P(), P()),
        out_specs=P("dp"),
        check_vma=False,
    )
```

```python
import functools

import jax
import jax.numpy as jnp
from jax import lax
from jax.experimental import pallas as pl
from jax.experimental.pallas import tpu as pltpu
from jax.sharding import PartitionSpec as P

CL_DEV = 32
LANES = 128
F32, BF16, I32 = jnp.float32, jnp.bfloat16, jnp.int32
VMEM = pl.BlockSpec(memory_space=pltpu.VMEM)
SMEM = pl.BlockSpec(memory_space=pltpu.SMEM)
AXES = ("dp", "mp")


def iota(shape, dimension):
    return lax.broadcasted_iota(I32, shape, dimension)


def dot(a, b):
    return lax.dot_general(a, b, (((1,), (0,)), ((), ())), preferred_element_type=F32)


def dot_nt(a, b):
    return lax.dot_general(a, b, (((1,), (1,)), ((), ())), preferred_element_type=F32)


def column(row):
    return jnp.transpose(jnp.broadcast_to(row, (LANES, LANES)))


def ones_where(mask):
    return jnp.where(mask, 1.0, 0.0)


def to_bf16(mask):
    return ones_where(mask).astype(BF16)


def earlier_lanes():
    return to_bf16(iota((LANES, LANES), 0) < iota((LANES, LANES), 1))


def owners_of(clusters):
    return lax.shift_right_logical(clusters, CL_DEV.bit_length() - 1)


def plan_kernel(dp_size, half, place, cluster_ref, target_ref, pair_ref, load_ref):
    owner_count = pair_ref.shape[0]
    tiles = target_ref.shape[0]
    wide = (owner_count, LANES)
    owner_ids = iota(wide, 0)
    ones = jnp.ones((LANES, LANES), BF16)
    owners = owners_of(cluster_ref[...])
    found = []
    for block in range(dp_size):
        counts = jnp.zeros(wide, F32)
        for tile in range(block * tiles, (block + 1) * tiles):
            counts = counts + ones_where(owner_ids == owners[tile : tile + 1, :])
        found.append(counts.astype(BF16))
    totals = dot(jnp.concatenate(found, axis=0), ones)
    totals = [totals[block * owner_count : (block + 1) * owner_count] for block in range(dp_size)]
    loads = sum(totals)
    square = (owner_count, owner_count)
    rows, columns = iota(square, 0), iota(square, 1)
    loads_column = loads[:, 0:1]
    loads_row = jnp.sum(jnp.where(rows == columns, loads_column, 0.0), axis=0, keepdims=True)
    lighter = (loads_row < loads_column) | ((loads_row == loads_column) & (columns < rows))
    position = dot(to_bf16(lighter), jnp.ones(wide, BF16))
    position_row = jnp.sum(jnp.where(rows == columns, position[:, 0:1], 0.0), axis=0, keepdims=True)
    partner = to_bf16(position_row == owner_count - 1 - position[:, 0:1])
    by_lane = sum(jnp.where(iota(wide, 1) == block, totals[block], 0.0) for block in range(dp_size))
    mine = sum(jnp.where(place[0] == block, totals[block], 0.0) for block in range(dp_size))
    both = dot(partner, jnp.concatenate([by_lane, mine], axis=1).astype(BF16))
    load_ref[...] = by_lane + both[:, :LANES]
    heavier = position >= owner_count // 2
    chip = jnp.where(heavier, owner_count - 1 - position, position)
    pair_ref[...] = jnp.where(chip == (place[1] // 2).astype(F32), jnp.where(heavier, 2.0, 1.0), 0.0)
    base = chip * (2 * half) + jnp.where(heavier, both[:, LANES:], 0.0)
    my_owners = owners_of(cluster_ref[pl.ds(pl.multiple_of(place[0] * tiles, 8), tiles), :])
    hits = [owner_ids == my_owners[tile : tile + 1, :] for tile in range(tiles)]
    stacked = jnp.concatenate([to_bf16(hit) for hit in hits], axis=0)
    counted = dot(stacked, jnp.concatenate([earlier_lanes(), ones], axis=1))
    for tile in range(tiles):
        span = slice(tile * owner_count, (tile + 1) * owner_count)
        slot = jnp.where(hits[tile], counted[span, :LANES] + base, 0.0)
        target_ref[tile : tile + 1, :] = jnp.sum(slot, axis=0, keepdims=True).astype(I32)
        base = base + counted[span, LANES:]


def pack_kernel(x_ref, target_ref, *refs):
    *sum_refs, out_ref, rows, picks = refs
    tiles = x_ref.shape[0] // LANES
    size = out_ref.shape[0]

    @pl.when(pl.program_id(0) == 0)
    def scale_rows():
        for tile in range(tiles):
            total = sum(ref[tile : tile + 1, :] for ref in sum_refs)
            scale = column(lax.rsqrt(total + 1e-06))
            span = slice(tile * LANES, (tile + 1) * LANES)
            for part in range(x_ref.shape[1] // LANES):
                lanes = slice(part * LANES, (part + 1) * LANES)
                rows[span, lanes] = (x_ref[span, lanes] * scale).astype(BF16)

    slot_ids = iota((LANES, LANES), 0).astype(BF16)
    for start in range(0, size, LANES):
        local = target_ref[...] - (pl.program_id(0) * size + start)
        local = jnp.where((local >= 0) & (local < LANES), local, -1).astype(F32)
        for tile in range(tiles):
            hit = slot_ids == local[tile : tile + 1, :].astype(BF16)
            picks[start : start + LANES, tile * LANES : (tile + 1) * LANES] = jnp.where(
                hit, jnp.ones((), BF16), jnp.zeros((), BF16)
            )
    out_ref[...] = dot(picks[...], rows[...]).astype(BF16)


def keys_kernel(dp_size, half, docs, place, cluster_ref, order_ref, pair_ref, row_ref, own_ref, other_ref):
    tiles = cluster_ref.shape[0]
    owner_count = pair_ref.shape[0]
    block_tiles = tiles // dp_size
    core = place[1] % 2
    code = pair_ref[:, 0:1]
    ids = iota((owner_count, 1), 0).astype(F32)
    owners = cluster_ref[...] // CL_DEV
    earlier = earlier_lanes()
    tile_row, tile_column = iota((tiles, tiles), 0), iota((tiles, tiles), 1)
    same_block = tile_column // block_tiles == tile_row // block_tiles
    before = to_bf16((tile_column < tile_row) & same_block)
    offset = jnp.zeros((tiles, LANES), F32)
    position = jnp.full((tiles, LANES), -1.0, F32)
    for which in (1.0, 2.0):
        owner = jnp.sum(jnp.where(code == which, ids, 0.0), axis=0, keepdims=True).astype(I32)
        mine = owners == owner
        totals = jnp.sum(ones_where(mine), axis=1, keepdims=True).astype(BF16)
        totals = jnp.broadcast_to(totals, (tiles, LANES))
        rank = dot(to_bf16(mine), earlier) + dot(before, totals) + offset
        position = jnp.where(mine, rank, position)
        offset = dot(to_bf16(same_block), totals)
    position = position.astype(I32)
    in_half = (position >= half).astype(I32)
    lane = jnp.where(position < 0, -1, position - in_half * half + jnp.where(in_half == core, 0, LANES))
    keys = cluster_ref[...] * docs + order_ref[...] + 1
    slot_ids = iota((2 * LANES, LANES), 0)
    for block in range(dp_size):
        total = jnp.zeros((8, 2 * LANES), F32)
        for tile in range(block * block_tiles, (block + 1) * block_tiles):
            key = keys[tile : tile + 1, :]
            pieces = [((key >> (8 * piece)) & 255).astype(F32) for piece in range(4)]
            pieces = jnp.concatenate(pieces + [jnp.zeros((4, LANES), F32)], axis=0).astype(BF16)
            total = total + dot_nt(pieces, to_bf16(slot_ids == lane[tile : tile + 1, :]))
        total = total.astype(I32)
        key = total[0:1] + (total[1:2] << 8) + (total[2:3] << 16) + (total[3:4] << 24) - 1
        for side, ref in enumerate((own_ref, other_ref)):
            ref[block * half : (block + 1) * half, :] = column(key[:, side * LANES : (side + 1) * LANES])[:half]
    for group in range(row_ref.shape[0]):
        row_ref[group : group + 1, :] = jnp.transpose(own_ref[group * LANES : (group + 1) * LANES, :])[0:1]


def pairs_kernel(docs, own_ref, early_ref, row_ref, column_ref, best_ref, out_ref):
    dp_size, mp_size, half, features = own_ref.shape
    slots = dp_size * half

    def whole(ref):
        parts = [ref[:, part].reshape(slots, features) for part in range(mp_size)]
        return jnp.concatenate(parts, axis=1)

    early = whole(early_ref)
    own = early if own_ref is early_ref else whole(own_ref)
    start, found = 0, []
    while start < slots:
        width = min(2 * LANES, slots - start)
        groups = range(start // LANES, (start + width) // LANES)
        key = jnp.concatenate([row_ref[group : group + 1, :] for group in groups], axis=1)
        lowest = jnp.where(key < 0, 0, (key // docs) * docs)
        cosines = dot_nt(early, own[start : start + width])
        keys = jnp.concatenate([column_ref[...]] * len(groups), axis=1)
        good = (keys >= lowest) & (keys < key)
        found.append(jnp.max(jnp.where(good, cosines, 0.0), axis=0, keepdims=True))
        start += width
    found = jnp.concatenate(found, axis=1)
    if best_ref is None:
        out_ref[...] = found
        return
    found = jnp.maximum(found, best_ref[...])
    for block in range(dp_size):
        out_ref[block] = jnp.broadcast_to(found[:, block * half : (block + 1) * half], (mp_size, half))


def own_pairs_kernel(docs, own_ref, row_ref, column_ref, out_ref):
    pairs_kernel(docs, own_ref, own_ref, row_ref, column_ref, None, out_ref)


def pick_kernel(results_ref, target_ref, out_ref):
    device_count, half = results_ref.shape
    tiles = target_ref.shape[0]
    results = results_ref[...]
    high = results.astype(BF16)
    rest = results - high.astype(F32)
    middle = rest.astype(BF16)
    low = (rest - middle.astype(F32)).astype(BF16)
    pieces = jnp.concatenate([high, middle, low], axis=0)
    device_ids = iota((device_count, LANES), 0)
    rank_ids = iota((half, LANES), 0)
    for tile in range(tiles):
        target = target_ref[tile : tile + 1, :]
        device = target // half
        one_hot = to_bf16(device_ids == device)
        one_hot = jnp.concatenate([one_hot, one_hot, one_hot], axis=0)
        ranked = lax.dot_general(pieces, one_hot, (((0,), (0,)), ((), ())), preferred_element_type=F32)
        hit = rank_ids == target - device * half
        out_ref[tile : tile + 1, :] = jnp.sum(jnp.where(hit, ranked, 0.0), axis=0, keepdims=True)


def call(kernel, out_shape, specs, out_specs=None, scratch=(), cost=0, megabytes=32):
    return pl.pallas_call(
        kernel,
        out_shape=out_shape,
        in_specs=specs,
        out_specs=out_specs or jax.tree.map(lambda _: VMEM, out_shape),
        scratch_shapes=list(scratch),
        compiler_params=pltpu.CompilerParams(vmem_limit_bytes=megabytes << 20),
        cost_estimate=pl.CostEstimate(flops=cost, bytes_accessed=1 << 20, transcendentals=0),
    )


def routed(half, place, embeddings, sums, clusters, orders):
    shape = jax.ShapeDtypeStruct
    block_rows, features = embeddings.shape
    docs = clusters.shape[0] * LANES
    dp_size, mp_size = lax.axis_size("dp"), lax.axis_size("mp")
    devices = dp_size * mp_size
    tiles = block_rows // LANES
    slots = dp_size * half
    targets, pair, loads = call(
        functools.partial(plan_kernel, dp_size, half),
        (shape((tiles, LANES), I32), *[shape((devices, LANES), F32)] * 2),
        [SMEM, VMEM],
        cost=10**8,
    )(place, clusters)
    size = max(size for size in range(LANES, 1281, LANES) if devices * half % size == 0)

    def whole(array):
        return pl.BlockSpec(array.shape, lambda step: (0, 0))

    packed = (embeddings, targets, *sums)
    outgoing = pl.pallas_call(
        pack_kernel,
        grid=(devices * half // size,),
        out_shape=shape((devices * half, features), BF16),
        in_specs=[whole(array) for array in packed],
        out_specs=pl.BlockSpec((size, features), lambda step: (step, 0)),
        scratch_shapes=[pltpu.VMEM((block_rows, features), BF16), pltpu.VMEM((size, block_rows), BF16)],
        compiler_params=pltpu.CompilerParams(vmem_limit_bytes=40 << 20),
    )(*packed)
    sources, outgoing = lax.optimization_barrier(((clusters, orders, pair), outgoing))
    arrived = lax.all_to_all(
        outgoing.reshape(devices, half, features), AXES, split_axis=0, concat_axis=0, tiled=True
    ).reshape(dp_size, mp_size, half, features)
    key_rows, own_columns, other_columns = call(
        functools.partial(keys_kernel, dp_size, half, docs),
        (shape((slots // LANES, LANES), I32), *[shape((slots, LANES), I32)] * 2),
        [SMEM, VMEM, VMEM, VMEM],
        cost=10**9,
    )(place, *sources)
    arrived, key_rows = lax.optimization_barrier((arrived, key_rows))
    other = lax.ppermute(arrived, "mp", [(i, i ^ 1) for i in range(mp_size)])
    work = 2 * slots * slots * features * mp_size
    best = call(functools.partial(own_pairs_kernel, docs), shape((1, slots), F32), [VMEM] * 3, cost=work)(
        arrived, key_rows, own_columns
    )
    highest = call(
        functools.partial(pairs_kernel, docs), shape((dp_size, mp_size, half), F32), [VMEM] * 5, cost=work
    )(arrived, other, key_rows, other_columns, best)
    results = lax.all_to_all(
        highest.reshape(devices, half), AXES, split_axis=0, concat_axis=0, tiled=True
    )
    return results, targets, jnp.max(loads) <= 2 * half


def pick(results, targets):
    picked = call(
        pick_kernel, jax.ShapeDtypeStruct(targets.shape, F32), [VMEM, VMEM], cost=10**8
    )(results, targets)
    return picked.reshape(targets.size)


def shards(embeddings, cluster_of, doc_order):
    block_rows, _ = embeddings.shape
    docs = cluster_of.shape[0]
    mp_size = lax.axis_size("mp")
    devices = lax.axis_size("dp") * mp_size
    most = 2 * block_rows // devices
    half = -(-5 * most // 8 // 16) * 16
    dp_index, mp_index = lax.axis_index("dp"), lax.axis_index("mp")
    place = jnp.stack([dp_index, dp_index * mp_size + mp_index]).astype(I32)
    clusters = cluster_of.reshape(docs // LANES, LANES)
    orders = doc_order.reshape(docs // LANES, LANES)
    squares = jnp.sum(embeddings * embeddings, axis=1).reshape(block_rows // LANES, LANES)
    others = [lax.ppermute(squares, "mp", [(i, i ^ k) for i in range(mp_size)]) for k in range(mp_size - 1, 0, -1)]
    sums = (squares, *others)
    arrays = (place, embeddings, sums, clusters, orders)
    results, targets, fits = routed(half, *arrays)
    if half == most:
        return pick(results, targets)
    return lax.cond(
        fits,
        lambda results, targets, *_: pick(results, targets),
        lambda _results, _targets, *rest: pick(*routed(most, *rest)[:2]),
        results,
        targets,
        *arrays,
    )


def solution(mesh):
    return jax.shard_map(
        shards,
        mesh=mesh,
        in_specs=(P("dp", "mp"), P(), P()),
        out_specs=P("dp"),
        check_vma=False,
    )
```

```python
import functools

import jax
import jax.numpy as jnp
from jax import lax
from jax.experimental import pallas as pl
from jax.experimental.pallas import tpu as pltpu
from jax.sharding import PartitionSpec as P

CL_DEV = 32
LANES = 128
F32, BF16, I32 = jnp.float32, jnp.bfloat16, jnp.int32
VMEM = pl.BlockSpec(memory_space=pltpu.VMEM)
SMEM = pl.BlockSpec(memory_space=pltpu.SMEM)
AXES = ("dp", "mp")


def iota(shape, dimension):
    return lax.broadcasted_iota(I32, shape, dimension)


def dot(a, b):
    return lax.dot_general(a, b, (((1,), (0,)), ((), ())), preferred_element_type=F32)


def dot_nt(a, b):
    return lax.dot_general(a, b, (((1,), (1,)), ((), ())), preferred_element_type=F32)


def column(row):
    return jnp.transpose(jnp.broadcast_to(row, (LANES, LANES)))


def ones_where(mask):
    return jnp.where(mask, 1.0, 0.0)


def to_bf16(mask):
    return ones_where(mask).astype(BF16)


def earlier_lanes():
    return to_bf16(iota((LANES, LANES), 0) < iota((LANES, LANES), 1))


def owners_of(clusters):
    return lax.shift_right_logical(clusters, CL_DEV.bit_length() - 1)


def plan_kernel(dp_size, half, place, cluster_ref, target_ref, pair_ref, load_ref):
    owner_count = pair_ref.shape[0]
    tiles = target_ref.shape[0]
    wide = (owner_count, LANES)
    owner_ids = iota(wide, 0)
    ones = jnp.ones((LANES, LANES), BF16)
    owners = owners_of(cluster_ref[...])
    found = []
    for block in range(dp_size):
        counts = jnp.zeros(wide, F32)
        for tile in range(block * tiles, (block + 1) * tiles):
            counts = counts + ones_where(owner_ids == owners[tile : tile + 1, :])
        found.append(counts.astype(BF16))
    totals = dot(jnp.concatenate(found, axis=0), ones)
    totals = [totals[block * owner_count : (block + 1) * owner_count] for block in range(dp_size)]
    loads = sum(totals)
    square = (owner_count, owner_count)
    rows, columns = iota(square, 0), iota(square, 1)
    loads_column = loads[:, 0:1]
    loads_row = jnp.sum(jnp.where(rows == columns, loads_column, 0.0), axis=0, keepdims=True)
    lighter = (loads_row < loads_column) | ((loads_row == loads_column) & (columns < rows))
    position = dot(to_bf16(lighter), jnp.ones(wide, BF16))
    position_row = jnp.sum(jnp.where(rows == columns, position[:, 0:1], 0.0), axis=0, keepdims=True)
    partner = to_bf16(position_row == owner_count - 1 - position[:, 0:1])
    by_lane = sum(jnp.where(iota(wide, 1) == block, totals[block], 0.0) for block in range(dp_size))
    mine = sum(jnp.where(place[0] == block, totals[block], 0.0) for block in range(dp_size))
    heavier = position >= owner_count // 2
    pair_load = by_lane + dot(partner, by_lane.astype(BF16))
    load_ref[...] = jnp.maximum(pair_load, jnp.where(heavier, 0.0, 2.0 * by_lane))
    chip = jnp.where(heavier, owner_count - 1 - position, position)
    pair_ref[...] = jnp.where(chip == (place[1] // 2).astype(F32), jnp.where(heavier, 2.0, 1.0), 0.0)
    base = chip * (2 * half) + jnp.where(heavier, 2 * half - mine, 0.0)
    my_owners = owners_of(cluster_ref[pl.ds(pl.multiple_of(place[0] * tiles, 8), tiles), :])
    hits = [owner_ids == my_owners[tile : tile + 1, :] for tile in range(tiles)]
    stacked = jnp.concatenate([to_bf16(hit) for hit in hits], axis=0)
    counted = dot(stacked, jnp.concatenate([earlier_lanes(), ones], axis=1))
    for tile in range(tiles):
        span = slice(tile * owner_count, (tile + 1) * owner_count)
        slot = jnp.where(hits[tile], counted[span, :LANES] + base, 0.0)
        target_ref[tile : tile + 1, :] = jnp.sum(slot, axis=0, keepdims=True).astype(I32)
        base = base + counted[span, LANES:]


def pack_kernel(x_ref, target_ref, *refs):
    *sum_refs, out_ref, rows, picks = refs
    tiles = x_ref.shape[0] // LANES
    size = out_ref.shape[0]

    @pl.when(pl.program_id(0) == 0)
    def scale_rows():
        for tile in range(tiles):
            total = sum(ref[tile : tile + 1, :] for ref in sum_refs)
            scale = column(lax.rsqrt(total + 1e-06))
            span = slice(tile * LANES, (tile + 1) * LANES)
            for part in range(x_ref.shape[1] // LANES):
                lanes = slice(part * LANES, (part + 1) * LANES)
                rows[span, lanes] = (x_ref[span, lanes] * scale).astype(BF16)

    slot_ids = iota((LANES, LANES), 0).astype(BF16)
    for start in range(0, size, LANES):
        local = target_ref[...] - (pl.program_id(0) * size + start)
        local = jnp.where((local >= 0) & (local < LANES), local, -1).astype(F32)
        for tile in range(tiles):
            hit = slot_ids == local[tile : tile + 1, :].astype(BF16)
            picks[start : start + LANES, tile * LANES : (tile + 1) * LANES] = jnp.where(
                hit, jnp.ones((), BF16), jnp.zeros((), BF16)
            )
    out_ref[...] = dot(picks[...], rows[...]).astype(BF16)


def keys_kernel(dp_size, half, window, docs, place, cluster_ref, order_ref, pair_ref, row_ref, own_ref, *window_ref):
    tiles = cluster_ref.shape[0]
    owner_count = pair_ref.shape[0]
    block_tiles = tiles // dp_size
    core = place[1] % 2
    code = pair_ref[:, 0:1]
    ids = iota((owner_count, 1), 0).astype(F32)
    owners = owners_of(cluster_ref[...])
    earlier = earlier_lanes()
    tile_row, tile_column = iota((tiles, tiles), 0), iota((tiles, tiles), 1)
    same_block = tile_column // block_tiles == tile_row // block_tiles
    before = to_bf16((tile_column < tile_row) & same_block)
    position = jnp.full((tiles, LANES), -1.0, F32)
    for which in (1.0, 2.0):
        owner = jnp.sum(jnp.where(code == which, ids, 0.0), axis=0, keepdims=True).astype(I32)
        mine = owners == owner
        totals = jnp.sum(ones_where(mine), axis=1, keepdims=True).astype(BF16)
        totals = jnp.broadcast_to(totals, (tiles, LANES))
        rank = dot(to_bf16(mine), earlier) + dot(before, totals)
        if which == 2.0:
            rank = rank + 2 * half - dot(to_bf16(same_block), totals)
        position = jnp.where(mine, rank, position)
    position = position.astype(I32)
    in_half = (position >= half).astype(I32)
    lane = jnp.where(position < 0, -1, position - in_half * half + jnp.where(in_half == core, 0, LANES))
    keys = cluster_ref[...] * docs + order_ref[...] + 1
    slot_ids = iota((2 * LANES, LANES), 0)
    for block in range(dp_size):
        total = jnp.zeros((8, 2 * LANES), F32)
        for tile in range(block * block_tiles, (block + 1) * block_tiles):
            key = keys[tile : tile + 1, :]
            pieces = [((key >> (8 * piece)) & 255).astype(F32) for piece in range(4)]
            pieces = jnp.concatenate(pieces + [jnp.zeros((4, LANES), F32)], axis=0).astype(BF16)
            total = total + dot_nt(pieces, to_bf16(slot_ids == lane[tile : tile + 1, :]))
        total = total.astype(I32)
        key = total[0:1] + (total[1:2] << 8) + (total[2:3] << 16) + (total[3:4] << 24) - 1
        own_ref[block * half : (block + 1) * half, :] = column(key[:, :LANES])[:half]
        if window:
            window_ref[0][block * window : (block + 1) * window, :] = column(key[:, LANES:])[half - window : half]
    for group in range(row_ref.shape[0]):
        row_ref[group : group + 1, :] = jnp.transpose(own_ref[group * LANES : (group + 1) * LANES, :])[0:1]


def whole_rows(ref):
    dp_size, mp_size, count, features = ref.shape
    return jnp.concatenate([ref[:, part].reshape(dp_size * count, features) for part in range(mp_size)], axis=1)


def lowest_key(key, docs):
    return jnp.where(key < 0, 0, (key // docs) * docs)


def column_groups(slots, row_ref):
    for start in range(0, slots, 2 * LANES):
        stop = min(start + 2 * LANES, slots)
        groups = range(start // LANES, stop // LANES)
        yield start, stop, jnp.concatenate([row_ref[group : group + 1, :] for group in groups], axis=1)


def own_pairs_kernel(docs, own_ref, row_ref, column_ref, out_ref):
    dp_size, mp_size, half, _ = own_ref.shape
    own = whole_rows(own_ref)
    found = []
    for start, stop, key in column_groups(own.shape[0], row_ref):
        cosines = dot_nt(own, own[start:stop])
        keys = jnp.concatenate([column_ref[...]] * ((stop - start) // LANES), axis=1)
        good = (keys >= lowest_key(key, docs)) & (keys < key)
        found.append(jnp.max(jnp.where(good, cosines, 0.0), axis=0, keepdims=True))
    found = jnp.concatenate(found, axis=1)
    if len(out_ref.shape) == 2:
        out_ref[...] = found
        return
    for block in range(dp_size):
        out_ref[block] = jnp.broadcast_to(found[:, block * half : (block + 1) * half], (mp_size, half))


def cross_pairs_kernel(docs, own_ref, window_ref, row_ref, column_ref, best_ref, out_ref):
    dp_size, mp_size, half, _ = own_ref.shape
    window = window_ref.shape[2]
    own, others = whole_rows(own_ref), whole_rows(window_ref)
    keys = column_ref[...]
    lowest = lowest_key(keys, docs)
    found, across = [], jnp.zeros(keys.shape, F32)
    for start, stop, key in column_groups(own.shape[0], row_ref):
        cosines = dot_nt(others, own[start:stop])
        my_lowest = lowest_key(key, docs)
        for at in range(0, stop - start, LANES):
            lanes = slice(at, at + LANES)
            mine, some = key[:, lanes], cosines[:, lanes]
            good = (keys >= my_lowest[:, lanes]) & (keys < mine)
            found.append(jnp.max(jnp.where(good, some, 0.0), axis=0, keepdims=True))
            good = (mine >= lowest) & (mine < keys)
            across = jnp.maximum(across, jnp.where(good, some, 0.0))
    found = jnp.maximum(jnp.concatenate(found, axis=1), best_ref[...])
    turned = [jnp.transpose(across[at : at + LANES]) for at in range(0, dp_size * window, LANES)]
    across = jnp.concatenate([jnp.max(part, axis=0, keepdims=True) for part in turned], axis=1)
    for block in range(dp_size):
        parts = (found[:, block * half : (block + 1) * half], across[:, block * window : (block + 1) * window])
        out_ref[block] = jnp.broadcast_to(jnp.concatenate(parts, axis=1), (mp_size, half + window))


def pick_kernel(half, results_ref, target_ref, out_ref):
    device_count, length = results_ref.shape
    tiles = target_ref.shape[0]
    results = results_ref[:, :half]
    window = length - half
    if window:
        across = jnp.concatenate([results_ref[1:, half:], results_ref[:1, half:]], axis=0)
        across = jnp.concatenate([jnp.zeros((device_count, half - window), F32), across], axis=1)
        results = jnp.where(iota(results.shape, 0) % 2 == 0, jnp.maximum(results, across), results)
    high = results.astype(BF16)
    rest = results - high.astype(F32)
    middle = rest.astype(BF16)
    low = (rest - middle.astype(F32)).astype(BF16)
    pieces = jnp.concatenate([high, middle, low], axis=0)
    device_ids = iota((device_count, LANES), 0)
    rank_ids = iota((half, LANES), 0)
    for tile in range(tiles):
        target = target_ref[tile : tile + 1, :]
        device = target // half
        one_hot = to_bf16(device_ids == device)
        one_hot = jnp.concatenate([one_hot, one_hot, one_hot], axis=0)
        ranked = lax.dot_general(pieces, one_hot, (((0,), (0,)), ((), ())), preferred_element_type=F32)
        hit = rank_ids == target - device * half
        out_ref[tile : tile + 1, :] = jnp.sum(jnp.where(hit, ranked, 0.0), axis=0, keepdims=True)


def call(kernel, out_shape, specs, out_specs=None, scratch=(), cost=0, megabytes=32):
    return pl.pallas_call(
        kernel,
        out_shape=out_shape,
        in_specs=specs,
        out_specs=out_specs or jax.tree.map(lambda _: VMEM, out_shape),
        scratch_shapes=list(scratch),
        compiler_params=pltpu.CompilerParams(vmem_limit_bytes=megabytes << 20),
        cost_estimate=pl.CostEstimate(flops=cost, bytes_accessed=1 << 20, transcendentals=0),
    )


def routed(half, place, embeddings, sums, clusters, orders):
    shape = jax.ShapeDtypeStruct
    block_rows, features = embeddings.shape
    docs = clusters.shape[0] * LANES
    dp_size, mp_size = lax.axis_size("dp"), lax.axis_size("mp")
    devices = dp_size * mp_size
    tiles = block_rows // LANES
    slots = dp_size * half
    window = 2 * block_rows // devices - half
    targets, pair, loads = call(
        functools.partial(plan_kernel, dp_size, half),
        (shape((tiles, LANES), I32), *[shape((devices, LANES), F32)] * 2),
        [SMEM, VMEM],
        cost=10**8,
    )(place, clusters)
    size = max(size for size in range(LANES, 1281, LANES) if devices * half % size == 0)

    def whole(array):
        return pl.BlockSpec(array.shape, lambda step: (0, 0))

    packed = (embeddings, targets, *sums)
    outgoing = pl.pallas_call(
        pack_kernel,
        grid=(devices * half // size,),
        out_shape=shape((devices * half, features), BF16),
        in_specs=[whole(array) for array in packed],
        out_specs=pl.BlockSpec((size, features), lambda step: (step, 0)),
        scratch_shapes=[pltpu.VMEM((block_rows, features), BF16), pltpu.VMEM((size, block_rows), BF16)],
        compiler_params=pltpu.CompilerParams(vmem_limit_bytes=40 << 20),
    )(*packed)
    sources, outgoing = lax.optimization_barrier(((clusters, orders, pair), outgoing))
    arrived = lax.all_to_all(
        outgoing.reshape(devices, half, features), AXES, split_axis=0, concat_axis=0, tiled=True
    ).reshape(dp_size, mp_size, half, features)
    columns = [shape((dp_size * count, LANES), I32) for count in (half, window) if count]
    key_rows, own_columns, *window_columns = call(
        functools.partial(keys_kernel, dp_size, half, window, docs),
        (shape((slots // LANES, LANES), I32), *columns),
        [SMEM, VMEM, VMEM, VMEM],
        cost=10**9,
    )(place, *sources)
    arrived, key_rows = lax.optimization_barrier((arrived, key_rows))
    work = 2 * slots * slots * features * mp_size
    best = call(
        functools.partial(own_pairs_kernel, docs),
        shape((1, slots) if window else (dp_size, mp_size, half), F32),
        [VMEM] * 3,
        cost=work,
    )(arrived, key_rows, own_columns)
    if window:
        other = lax.ppermute(arrived[:, :, half - window :], "mp", [(i, i ^ 1) for i in range(mp_size)])
        best = call(
            functools.partial(cross_pairs_kernel, docs),
            shape((dp_size, mp_size, half + window), F32),
            [VMEM] * 5,
            cost=work,
        )(arrived, other, key_rows, window_columns[0], best)
    results = lax.all_to_all(
        best.reshape(devices, half + window), AXES, split_axis=0, concat_axis=0, tiled=True
    )
    return results, targets, jnp.max(loads) <= 2 * half


def pick(half, results, targets):
    picked = call(
        functools.partial(pick_kernel, half), jax.ShapeDtypeStruct(targets.shape, F32), [VMEM, VMEM], cost=10**8
    )(results, targets)
    return picked.reshape(targets.size)


def shards(embeddings, cluster_of, doc_order):
    block_rows, _ = embeddings.shape
    docs = cluster_of.shape[0]
    mp_size = lax.axis_size("mp")
    devices = lax.axis_size("dp") * mp_size
    most = 2 * block_rows // devices
    half = -(-5 * most // 8 // 16) * 16
    dp_size = lax.axis_size("dp")
    if dp_size * half % LANES or dp_size * (most - half) % LANES:
        half = most
    dp_index, mp_index = lax.axis_index("dp"), lax.axis_index("mp")
    place = jnp.stack([dp_index, dp_index * mp_size + mp_index]).astype(I32)
    clusters = cluster_of.reshape(docs // LANES, LANES)
    orders = doc_order.reshape(docs // LANES, LANES)
    squares = jnp.sum(embeddings * embeddings, axis=1).reshape(block_rows // LANES, LANES)
    others = [lax.ppermute(squares, "mp", [(i, i ^ k) for i in range(mp_size)]) for k in range(mp_size - 1, 0, -1)]
    sums = (squares, *others)
    arrays = (place, embeddings, sums, clusters, orders)
    results, targets, fits = routed(half, *arrays)
    if half == most:
        return pick(half, results, targets)
    return lax.cond(
        fits,
        lambda results, targets, *_: pick(half, results, targets),
        lambda _results, _targets, *rest: pick(most, *routed(most, *rest)[:2]),
        results,
        targets,
        *arrays,
    )


def solution(mesh):
    return jax.shard_map(
        shards,
        mesh=mesh,
        in_specs=(P("dp", "mp"), P(), P()),
        out_specs=P("dp"),
        check_vma=False,
    )
```

```python
import functools

import jax
import jax.numpy as jnp
from jax import lax
from jax.experimental import pallas as pl
from jax.experimental.pallas import tpu as pltpu
from jax.sharding import PartitionSpec as P

CL_DEV = 32
LANES = 128
F32, BF16, I32 = jnp.float32, jnp.bfloat16, jnp.int32
VMEM = pl.BlockSpec(memory_space=pltpu.VMEM)
SMEM = pl.BlockSpec(memory_space=pltpu.SMEM)
AXES = ("dp", "mp")


def iota(shape, dimension):
    return lax.broadcasted_iota(I32, shape, dimension)


def dot(a, b):
    return lax.dot_general(a, b, (((1,), (0,)), ((), ())), preferred_element_type=F32)


def dot_nt(a, b):
    return lax.dot_general(a, b, (((1,), (1,)), ((), ())), preferred_element_type=F32)


def column(row):
    return jnp.transpose(jnp.broadcast_to(row, (LANES, LANES)))


def ones_where(mask):
    return jnp.where(mask, 1.0, 0.0)


def to_bf16(mask):
    return ones_where(mask).astype(BF16)


def earlier_lanes():
    return to_bf16(iota((LANES, LANES), 0) < iota((LANES, LANES), 1))


def owners_of(clusters):
    return lax.shift_right_logical(clusters, CL_DEV.bit_length() - 1)


def plan_kernel(dp_size, half, place, cluster_ref, target_ref, pair_ref, load_ref):
    owner_count = pair_ref.shape[0]
    tiles = target_ref.shape[0]
    wide = (owner_count, LANES)
    owner_ids = iota(wide, 0)
    ones = jnp.ones((LANES, LANES), BF16)
    owners = owners_of(cluster_ref[...])
    found = []
    for block in range(dp_size):
        counts = jnp.zeros(wide, F32)
        for tile in range(block * tiles, (block + 1) * tiles):
            counts = counts + ones_where(owner_ids == owners[tile : tile + 1, :])
        found.append(counts.astype(BF16))
    totals = dot(jnp.concatenate(found, axis=0), ones)
    totals = [totals[block * owner_count : (block + 1) * owner_count] for block in range(dp_size)]
    loads = sum(totals)
    square = (owner_count, owner_count)
    rows, columns = iota(square, 0), iota(square, 1)
    loads_column = loads[:, 0:1]
    loads_row = jnp.sum(jnp.where(rows == columns, loads_column, 0.0), axis=0, keepdims=True)
    lighter = (loads_row < loads_column) | ((loads_row == loads_column) & (columns < rows))
    position = dot(to_bf16(lighter), jnp.ones(wide, BF16))
    position_row = jnp.sum(jnp.where(rows == columns, position[:, 0:1], 0.0), axis=0, keepdims=True)
    partner = to_bf16(position_row == owner_count - 1 - position[:, 0:1])
    by_lane = sum(jnp.where(iota(wide, 1) == block, totals[block], 0.0) for block in range(dp_size))
    mine = sum(jnp.where(place[0] == block, totals[block], 0.0) for block in range(dp_size))
    heavier = position >= owner_count // 2
    pair_load = by_lane + dot(partner, by_lane.astype(BF16))
    load_ref[...] = jnp.maximum(pair_load, jnp.where(heavier, 0.0, 2.0 * by_lane))
    chip = jnp.where(heavier, owner_count - 1 - position, position)
    pair_ref[...] = jnp.where(chip == (place[1] // 2).astype(F32), jnp.where(heavier, 2.0, 1.0), 0.0)
    base = chip * (2 * half) + jnp.where(heavier, 2 * half - mine, 0.0)
    my_owners = owners_of(cluster_ref[pl.ds(pl.multiple_of(place[0] * tiles, 8), tiles), :])
    hits = [owner_ids == my_owners[tile : tile + 1, :] for tile in range(tiles)]
    stacked = jnp.concatenate([to_bf16(hit) for hit in hits], axis=0)
    counted = dot(stacked, jnp.concatenate([earlier_lanes(), ones], axis=1))
    for tile in range(tiles):
        span = slice(tile * owner_count, (tile + 1) * owner_count)
        slot = jnp.where(hits[tile], counted[span, :LANES] + base, 0.0)
        target_ref[tile : tile + 1, :] = jnp.sum(slot, axis=0, keepdims=True).astype(I32)
        base = base + counted[span, LANES:]


def pack_kernel(x_ref, target_ref, *refs):
    *sum_refs, out_ref, rows, picks = refs
    tiles = x_ref.shape[0] // LANES
    size = out_ref.shape[0]

    @pl.when(pl.program_id(0) == 0)
    def scale_rows():
        for tile in range(tiles):
            total = sum(ref[tile : tile + 1, :] for ref in sum_refs)
            scale = column(lax.rsqrt(total + 1e-06))
            span = slice(tile * LANES, (tile + 1) * LANES)
            for part in range(x_ref.shape[1] // LANES):
                lanes = slice(part * LANES, (part + 1) * LANES)
                rows[span, lanes] = (x_ref[span, lanes] * scale).astype(BF16)

    slot_ids = iota((LANES, LANES), 0).astype(BF16)
    for start in range(0, size, LANES):
        local = target_ref[...] - (pl.program_id(0) * size + start)
        local = jnp.where((local >= 0) & (local < LANES), local, -1).astype(F32)
        for tile in range(tiles):
            hit = slot_ids == local[tile : tile + 1, :].astype(BF16)
            picks[start : start + LANES, tile * LANES : (tile + 1) * LANES] = jnp.where(
                hit, jnp.ones((), BF16), jnp.zeros((), BF16)
            )
    out_ref[...] = dot(picks[...], rows[...]).astype(BF16)


def keys_kernel(dp_size, half, window, docs, place, cluster_ref, order_ref, pair_ref, row_ref, own_ref, *window_ref):
    tiles = cluster_ref.shape[0]
    owner_count = pair_ref.shape[0]
    block_tiles = tiles // dp_size
    core = place[1] % 2
    code = pair_ref[:, 0:1]
    ids = iota((owner_count, 1), 0).astype(F32)
    owners = owners_of(cluster_ref[...])
    earlier = earlier_lanes()
    tile_row, tile_column = iota((tiles, tiles), 0), iota((tiles, tiles), 1)
    same_block = tile_column // block_tiles == tile_row // block_tiles
    before = to_bf16((tile_column < tile_row) & same_block)
    position = jnp.full((tiles, LANES), -1.0, F32)
    for which in (1.0, 2.0):
        owner = jnp.sum(jnp.where(code == which, ids, 0.0), axis=0, keepdims=True).astype(I32)
        mine = owners == owner
        totals = jnp.sum(ones_where(mine), axis=1, keepdims=True).astype(BF16)
        totals = jnp.broadcast_to(totals, (tiles, LANES))
        rank = dot(to_bf16(mine), earlier) + dot(before, totals)
        if which == 2.0:
            rank = rank + 2 * half - dot(to_bf16(same_block), totals)
        position = jnp.where(mine, rank, position)
    position = position.astype(I32)
    in_half = (position >= half).astype(I32)
    lane = jnp.where(position < 0, -1, position - in_half * half + jnp.where(in_half == core, 0, LANES))
    keys = cluster_ref[...] * docs + order_ref[...] + 1
    slot_ids = iota((2 * LANES, LANES), 0)
    for block in range(dp_size):
        total = jnp.zeros((8, 2 * LANES), F32)
        for tile in range(block * block_tiles, (block + 1) * block_tiles):
            key = keys[tile : tile + 1, :]
            pieces = [((key >> (8 * piece)) & 255).astype(F32) for piece in range(4)]
            pieces = jnp.concatenate(pieces + [jnp.zeros((4, LANES), F32)], axis=0).astype(BF16)
            total = total + dot_nt(pieces, to_bf16(slot_ids == lane[tile : tile + 1, :]))
        total = total.astype(I32)
        key = total[0:1] + (total[1:2] << 8) + (total[2:3] << 16) + (total[3:4] << 24) - 1
        own_ref[block * half : (block + 1) * half, :] = column(key[:, :LANES])[:half]
        if window:
            window_ref[0][block * window : (block + 1) * window, :] = column(key[:, LANES:])[half - window : half]
    for group in range(row_ref.shape[0]):
        row_ref[group : group + 1, :] = jnp.transpose(own_ref[group * LANES : (group + 1) * LANES, :])[0:1]


def whole_rows(ref):
    dp_size, mp_size, count, features = ref.shape
    return jnp.concatenate([ref[:, part].reshape(dp_size * count, features) for part in range(mp_size)], axis=1)


def lowest_key(key, docs):
    return jnp.where(key < 0, 0, (key // docs) * docs)


def column_groups(slots, row_ref):
    for start in range(0, slots, 2 * LANES):
        stop = min(start + 2 * LANES, slots)
        groups = range(start // LANES, stop // LANES)
        yield start, stop, jnp.concatenate([row_ref[group : group + 1, :] for group in groups], axis=1)


def own_pairs_kernel(docs, own_ref, row_ref, column_ref, out_ref):
    dp_size, mp_size, half, _ = own_ref.shape
    own = whole_rows(own_ref)
    found = []
    for start, stop, key in column_groups(own.shape[0], row_ref):
        cosines = dot_nt(own, own[start:stop])
        keys = jnp.concatenate([column_ref[...]] * ((stop - start) // LANES), axis=1)
        good = (keys >= lowest_key(key, docs)) & (keys < key)
        found.append(jnp.max(jnp.where(good, cosines, 0.0), axis=0, keepdims=True))
    found = jnp.concatenate(found, axis=1)
    if len(out_ref.shape) == 2:
        out_ref[...] = found
        return
    for block in range(dp_size):
        out_ref[block] = jnp.broadcast_to(found[:, block * half : (block + 1) * half], (mp_size, half))


def cross_pairs_kernel(docs, own_ref, window_ref, row_ref, column_ref, best_ref, out_ref):
    dp_size, mp_size, half, _ = own_ref.shape
    window = window_ref.shape[2]
    own, others = whole_rows(own_ref), whole_rows(window_ref)
    keys = column_ref[...]
    lowest = lowest_key(keys, docs)
    found, across = [], jnp.zeros(keys.shape, F32)
    for start, stop, key in column_groups(own.shape[0], row_ref):
        cosines = dot_nt(others, own[start:stop])
        my_lowest = lowest_key(key, docs)
        for at in range(0, stop - start, LANES):
            lanes = slice(at, at + LANES)
            mine, some = key[:, lanes], cosines[:, lanes]
            good = (keys >= my_lowest[:, lanes]) & (keys < mine)
            found.append(jnp.max(jnp.where(good, some, 0.0), axis=0, keepdims=True))
            good = (mine >= lowest) & (mine < keys)
            across = jnp.maximum(across, jnp.where(good, some, 0.0))
    found = jnp.maximum(jnp.concatenate(found, axis=1), best_ref[...])
    turned = [jnp.transpose(across[at : at + LANES]) for at in range(0, dp_size * window, LANES)]
    across = jnp.concatenate([jnp.max(part, axis=0, keepdims=True) for part in turned], axis=1)
    for block in range(dp_size):
        parts = (found[:, block * half : (block + 1) * half], across[:, block * window : (block + 1) * window])
        out_ref[block] = jnp.broadcast_to(jnp.concatenate(parts, axis=1), (mp_size, half + window))


def pick_kernel(half, results_ref, target_ref, out_ref):
    device_count, length = results_ref.shape
    tiles = target_ref.shape[0]
    results = results_ref[:, :half]
    window = length - half
    if window:
        across = jnp.concatenate([results_ref[1:, half:], results_ref[:1, half:]], axis=0)
        across = jnp.concatenate([jnp.zeros((device_count, half - window), F32), across], axis=1)
        results = jnp.where(iota(results.shape, 0) % 2 == 0, jnp.maximum(results, across), results)
    high = results.astype(BF16)
    rest = results - high.astype(F32)
    middle = rest.astype(BF16)
    low = (rest - middle.astype(F32)).astype(BF16)
    pieces = jnp.concatenate([high, middle, low], axis=0)
    device_ids = iota((device_count, LANES), 0)
    rank_ids = iota((half, LANES), 0)
    for tile in range(tiles):
        target = target_ref[tile : tile + 1, :]
        device = target // half
        one_hot = to_bf16(device_ids == device)
        one_hot = jnp.concatenate([one_hot, one_hot, one_hot], axis=0)
        ranked = lax.dot_general(pieces, one_hot, (((0,), (0,)), ((), ())), preferred_element_type=F32)
        hit = rank_ids == target - device * half
        out_ref[tile : tile + 1, :] = jnp.sum(jnp.where(hit, ranked, 0.0), axis=0, keepdims=True)


def call(kernel, out_shape, specs, out_specs=None, scratch=(), cost=0, megabytes=32):
    return pl.pallas_call(
        kernel,
        out_shape=out_shape,
        in_specs=specs,
        out_specs=out_specs or jax.tree.map(lambda _: VMEM, out_shape),
        scratch_shapes=list(scratch),
        compiler_params=pltpu.CompilerParams(vmem_limit_bytes=megabytes << 20),
        cost_estimate=pl.CostEstimate(flops=cost, bytes_accessed=1 << 20, transcendentals=0),
    )


def routed(half, place, embeddings, sums, clusters, orders):
    shape = jax.ShapeDtypeStruct
    block_rows, features = embeddings.shape
    docs = clusters.shape[0] * LANES
    dp_size, mp_size = lax.axis_size("dp"), lax.axis_size("mp")
    devices = dp_size * mp_size
    tiles = block_rows // LANES
    slots = dp_size * half
    window = 2 * block_rows // devices - half
    targets, pair, loads = call(
        functools.partial(plan_kernel, dp_size, half),
        (shape((tiles, LANES), I32), *[shape((devices, LANES), F32)] * 2),
        [SMEM, VMEM],
        cost=10**8,
    )(place, clusters)
    size = max(size for size in range(LANES, 1281, LANES) if devices * half % size == 0)

    def whole(array):
        return pl.BlockSpec(array.shape, lambda step: (0, 0))

    packed = (embeddings, targets, *sums)
    outgoing = pl.pallas_call(
        pack_kernel,
        grid=(devices * half // size,),
        out_shape=shape((devices * half, features), BF16),
        in_specs=[whole(array) for array in packed],
        out_specs=pl.BlockSpec((size, features), lambda step: (step, 0)),
        scratch_shapes=[pltpu.VMEM((block_rows, features), BF16), pltpu.VMEM((size, block_rows), BF16)],
        compiler_params=pltpu.CompilerParams(vmem_limit_bytes=40 << 20),
    )(*packed)
    sources, outgoing = lax.optimization_barrier(((clusters, orders, pair), outgoing))
    arrived = lax.all_to_all(
        outgoing.reshape(devices, half, features), AXES, split_axis=0, concat_axis=0, tiled=True
    ).reshape(dp_size, mp_size, half, features)
    columns = [shape((dp_size * count, LANES), I32) for count in (half, window) if count]
    key_rows, own_columns, *window_columns = call(
        functools.partial(keys_kernel, dp_size, half, window, docs),
        (shape((slots // LANES, LANES), I32), *columns),
        [SMEM, VMEM, VMEM, VMEM],
        cost=10**9,
    )(place, *sources)
    fits = (jnp.max(loads) <= 2 * half).astype(I32)
    arrived, key_rows, fits = lax.optimization_barrier((arrived, key_rows, fits))
    work = 2 * slots * slots * features * mp_size
    best = call(
        functools.partial(own_pairs_kernel, docs),
        shape((1, slots) if window else (dp_size, mp_size, half), F32),
        [VMEM] * 3,
        cost=work,
    )(arrived, key_rows, own_columns)
    if window:
        other = lax.ppermute(arrived[:, :, half - window :], "mp", [(i, i ^ 1) for i in range(mp_size)])
        best = call(
            functools.partial(cross_pairs_kernel, docs),
            shape((dp_size, mp_size, half + window), F32),
            [VMEM] * 5,
            cost=work,
        )(arrived, other, key_rows, window_columns[0], best)
    results = lax.all_to_all(
        best.reshape(devices, half + window), AXES, split_axis=0, concat_axis=0, tiled=True
    )
    return results, targets, fits


def pick(half, results, targets):
    picked = call(
        functools.partial(pick_kernel, half), jax.ShapeDtypeStruct(targets.shape, F32), [VMEM, VMEM], cost=10**8
    )(results, targets)
    return picked.reshape(targets.size)


def shards(embeddings, cluster_of, doc_order):
    block_rows, _ = embeddings.shape
    docs = cluster_of.shape[0]
    mp_size = lax.axis_size("mp")
    devices = lax.axis_size("dp") * mp_size
    most = 2 * block_rows // devices
    half = -(-5 * most // 8 // 16) * 16
    dp_size = lax.axis_size("dp")
    if dp_size * half % LANES or dp_size * (most - half) % LANES:
        half = most
    dp_index, mp_index = lax.axis_index("dp"), lax.axis_index("mp")
    place = jnp.stack([dp_index, dp_index * mp_size + mp_index]).astype(I32)
    clusters = cluster_of.reshape(docs // LANES, LANES)
    orders = doc_order.reshape(docs // LANES, LANES)
    squares = jnp.sum(embeddings * embeddings, axis=1).reshape(block_rows // LANES, LANES)
    others = [lax.ppermute(squares, "mp", [(i, i ^ k) for i in range(mp_size)]) for k in range(mp_size - 1, 0, -1)]
    sums = (squares, *others)
    arrays = (place, embeddings, sums, clusters, orders)
    results, targets, fits = routed(half, *arrays)
    if half == most:
        return pick(half, results, targets)
    return lax.cond(
        fits,
        lambda results, targets, *_: pick(half, results, targets),
        lambda _results, _targets, *rest: pick(most, *routed(most, *rest)[:2]),
        results,
        targets,
        *arrays,
    )


def solution(mesh):
    return jax.shard_map(
        shards,
        mesh=mesh,
        in_specs=(P("dp", "mp"), P(), P()),
        out_specs=P("dp"),
        check_vma=False,
    )
```

```python
import functools

import jax
import jax.numpy as jnp
from jax import lax
from jax.experimental import pallas as pl
from jax.experimental.pallas import tpu as pltpu
from jax.sharding import PartitionSpec as P

CL_DEV = 32
LANES = 128
F32, BF16, I32 = jnp.float32, jnp.bfloat16, jnp.int32
VMEM = pl.BlockSpec(memory_space=pltpu.VMEM)
SMEM = pl.BlockSpec(memory_space=pltpu.SMEM)
AXES = ("dp", "mp")


def iota(shape, dimension):
    return lax.broadcasted_iota(I32, shape, dimension)


def dot(a, b):
    return lax.dot_general(a, b, (((1,), (0,)), ((), ())), preferred_element_type=F32)


def dot_nt(a, b):
    return lax.dot_general(a, b, (((1,), (1,)), ((), ())), preferred_element_type=F32)


def column(row):
    return jnp.transpose(jnp.broadcast_to(row, (LANES, LANES)))


def ones_where(mask):
    return jnp.where(mask, 1.0, 0.0)


def to_bf16(mask):
    return ones_where(mask).astype(BF16)


def earlier_lanes():
    return to_bf16(iota((LANES, LANES), 0) < iota((LANES, LANES), 1))


def squares_kernel(x_ref, cluster_ref, sum_ref, kept_ref, rows_ref, arrived):
    pieces = arrived.shape[0] - 1
    size = x_ref.shape[0] // pieces
    copies = []
    for piece in range(pieces):
        span = pl.ds(piece * size, size)
        copies.append(pltpu.make_async_copy(x_ref.at[span, :], rows_ref.at[span, :], arrived.at[piece]))
    copies.append(pltpu.make_async_copy(cluster_ref, kept_ref, arrived.at[pieces]))
    for copy in copies:
        copy.start()
    for piece in range(pieces):
        copies[piece].wait()
        for tile in range(piece * size // LANES, (piece + 1) * size // LANES):
            x = rows_ref[tile * LANES : (tile + 1) * LANES, :]
            x = sum(x[:, lane : lane + LANES] * x[:, lane : lane + LANES] for lane in range(0, x.shape[1], LANES))
            sum_ref[tile : tile + 1, :] = jnp.sum(jnp.transpose(x), axis=0, keepdims=True)
    copies[pieces].wait()


def owners_of(clusters):
    return lax.shift_right_logical(clusters, CL_DEV.bit_length() - 1)


def plan_kernel(dp_size, half, place, cluster_ref, target_ref, pair_ref, load_ref):
    owner_count = pair_ref.shape[0]
    tiles = target_ref.shape[0]
    wide = (owner_count, LANES)
    owner_ids = iota(wide, 0)
    ones = jnp.ones((LANES, LANES), BF16)
    owners = owners_of(cluster_ref[...])
    found = []
    for block in range(dp_size):
        counts = jnp.zeros(wide, F32)
        for tile in range(block * tiles, (block + 1) * tiles):
            counts = counts + ones_where(owner_ids == owners[tile : tile + 1, :])
        found.append(counts.astype(BF16))
    totals = dot(jnp.concatenate(found, axis=0), ones)
    totals = [totals[block * owner_count : (block + 1) * owner_count] for block in range(dp_size)]
    loads = sum(totals)
    square = (owner_count, owner_count)
    rows, columns = iota(square, 0), iota(square, 1)
    loads_column = loads[:, 0:1]
    loads_row = jnp.sum(jnp.where(rows == columns, loads_column, 0.0), axis=0, keepdims=True)
    lighter = (loads_row < loads_column) | ((loads_row == loads_column) & (columns < rows))
    position = dot(to_bf16(lighter), jnp.ones(wide, BF16))
    position_row = jnp.sum(jnp.where(rows == columns, position[:, 0:1], 0.0), axis=0, keepdims=True)
    partner = to_bf16(position_row == owner_count - 1 - position[:, 0:1])
    by_lane = sum(jnp.where(iota(wide, 1) == block, totals[block], 0.0) for block in range(dp_size))
    mine = sum(jnp.where(place[0] == block, totals[block], 0.0) for block in range(dp_size))
    heavier = position >= owner_count // 2
    pair_load = by_lane + dot(partner, by_lane.astype(BF16))
    load_ref[...] = jnp.maximum(pair_load, jnp.where(heavier, 0.0, 2.0 * by_lane))
    chip = jnp.where(heavier, owner_count - 1 - position, position)
    pair_ref[...] = jnp.where(chip == (place[1] // 2).astype(F32), jnp.where(heavier, 2.0, 1.0), 0.0)
    base = chip * (2 * half) + jnp.where(heavier, 2 * half - mine, 0.0)
    my_owners = owners_of(cluster_ref[pl.ds(pl.multiple_of(place[0] * tiles, 8), tiles), :])
    hits = [owner_ids == my_owners[tile : tile + 1, :] for tile in range(tiles)]
    stacked = jnp.concatenate([to_bf16(hit) for hit in hits], axis=0)
    counted = dot(stacked, jnp.concatenate([earlier_lanes(), ones], axis=1))
    for tile in range(tiles):
        span = slice(tile * owner_count, (tile + 1) * owner_count)
        slot = jnp.where(hits[tile], counted[span, :LANES] + base, 0.0)
        target_ref[tile : tile + 1, :] = jnp.sum(slot, axis=0, keepdims=True).astype(I32)
        base = base + counted[span, LANES:]


def pack_kernel(x_ref, target_ref, *refs):
    *sum_refs, out_ref, rows, picks = refs
    tiles = x_ref.shape[0] // LANES
    size = out_ref.shape[0]

    @pl.when(pl.program_id(0) == 0)
    def scale_rows():
        for tile in range(tiles):
            total = sum(ref[tile : tile + 1, :] for ref in sum_refs)
            scale = column(lax.rsqrt(total + 1e-06))
            span = slice(tile * LANES, (tile + 1) * LANES)
            for part in range(x_ref.shape[1] // LANES):
                lanes = slice(part * LANES, (part + 1) * LANES)
                rows[span, lanes] = (x_ref[span, lanes] * scale).astype(BF16)

    slot_ids = iota((LANES, LANES), 0).astype(BF16)
    for start in range(0, size, LANES):
        local = target_ref[...] - (pl.program_id(0) * size + start)
        local = jnp.where((local >= 0) & (local < LANES), local, -1).astype(F32)
        for tile in range(tiles):
            hit = slot_ids == local[tile : tile + 1, :].astype(BF16)
            picks[start : start + LANES, tile * LANES : (tile + 1) * LANES] = jnp.where(
                hit, jnp.ones((), BF16), jnp.zeros((), BF16)
            )
    out_ref[...] = dot(picks[...], rows[...]).astype(BF16)


def keys_kernel(dp_size, half, window, docs, place, cluster_ref, order_ref, pair_ref, row_ref, own_ref, *window_ref):
    tiles = cluster_ref.shape[0]
    owner_count = pair_ref.shape[0]
    block_tiles = tiles // dp_size
    core = place[1] % 2
    code = pair_ref[:, 0:1]
    ids = iota((owner_count, 1), 0).astype(F32)
    owners = owners_of(cluster_ref[...])
    earlier = earlier_lanes()
    tile_row, tile_column = iota((tiles, tiles), 0), iota((tiles, tiles), 1)
    same_block = tile_column // block_tiles == tile_row // block_tiles
    before = to_bf16((tile_column < tile_row) & same_block)
    position = jnp.full((tiles, LANES), -1.0, F32)
    for which in (1.0, 2.0):
        owner = jnp.sum(jnp.where(code == which, ids, 0.0), axis=0, keepdims=True).astype(I32)
        mine = owners == owner
        totals = jnp.sum(ones_where(mine), axis=1, keepdims=True).astype(BF16)
        totals = jnp.broadcast_to(totals, (tiles, LANES))
        rank = dot(to_bf16(mine), earlier) + dot(before, totals)
        if which == 2.0:
            rank = rank + 2 * half - dot(to_bf16(same_block), totals)
        position = jnp.where(mine, rank, position)
    position = position.astype(I32)
    in_half = (position >= half).astype(I32)
    lane = jnp.where(position < 0, -1, position - in_half * half + jnp.where(in_half == core, 0, LANES))
    keys = cluster_ref[...] * docs + order_ref[...] + 1
    slot_ids = iota((2 * LANES, LANES), 0)
    for block in range(dp_size):
        total = jnp.zeros((8, 2 * LANES), F32)
        for tile in range(block * block_tiles, (block + 1) * block_tiles):
            key = keys[tile : tile + 1, :]
            pieces = [((key >> (8 * piece)) & 255).astype(F32) for piece in range(4)]
            pieces = jnp.concatenate(pieces + [jnp.zeros((4, LANES), F32)], axis=0).astype(BF16)
            total = total + dot_nt(pieces, to_bf16(slot_ids == lane[tile : tile + 1, :]))
        total = total.astype(I32)
        key = total[0:1] + (total[1:2] << 8) + (total[2:3] << 16) + (total[3:4] << 24) - 1
        own_ref[block * half : (block + 1) * half, :] = column(key[:, :LANES])[:half]
        if window:
            window_ref[0][block * window : (block + 1) * window, :] = column(key[:, LANES:])[half - window : half]
    for group in range(row_ref.shape[0]):
        row_ref[group : group + 1, :] = jnp.transpose(own_ref[group * LANES : (group + 1) * LANES, :])[0:1]


def whole_rows(ref):
    dp_size, mp_size, count, features = ref.shape
    return jnp.concatenate([ref[:, part].reshape(dp_size * count, features) for part in range(mp_size)], axis=1)


def lowest_key(key, docs):
    return jnp.where(key < 0, 0, (key // docs) * docs)


def column_groups(slots, row_ref):
    for start in range(0, slots, 2 * LANES):
        stop = min(start + 2 * LANES, slots)
        groups = range(start // LANES, stop // LANES)
        yield start, stop, jnp.concatenate([row_ref[group : group + 1, :] for group in groups], axis=1)


def own_pairs_kernel(docs, own_ref, row_ref, column_ref, out_ref):
    dp_size, mp_size, half, _ = own_ref.shape
    own = whole_rows(own_ref)
    found = []
    for start, stop, key in column_groups(own.shape[0], row_ref):
        cosines = dot_nt(own, own[start:stop])
        keys = jnp.concatenate([column_ref[...]] * ((stop - start) // LANES), axis=1)
        good = (keys >= lowest_key(key, docs)) & (keys < key)
        found.append(jnp.max(jnp.where(good, cosines, 0.0), axis=0, keepdims=True))
    found = jnp.concatenate(found, axis=1)
    if len(out_ref.shape) == 2:
        out_ref[...] = found
        return
    for block in range(dp_size):
        out_ref[block] = jnp.broadcast_to(found[:, block * half : (block + 1) * half], (mp_size, half))


def cross_pairs_kernel(docs, own_ref, window_ref, row_ref, column_ref, best_ref, out_ref):
    dp_size, mp_size, half, _ = own_ref.shape
    window = window_ref.shape[2]
    own, others = whole_rows(own_ref), whole_rows(window_ref)
    keys = column_ref[...]
    lowest = lowest_key(keys, docs)
    found, across = [], jnp.zeros(keys.shape, F32)
    for start, stop, key in column_groups(own.shape[0], row_ref):
        cosines = dot_nt(others, own[start:stop])
        my_lowest = lowest_key(key, docs)
        for at in range(0, stop - start, LANES):
            lanes = slice(at, at + LANES)
            mine, some = key[:, lanes], cosines[:, lanes]
            good = (keys >= my_lowest[:, lanes]) & (keys < mine)
            found.append(jnp.max(jnp.where(good, some, 0.0), axis=0, keepdims=True))
            good = (mine >= lowest) & (mine < keys)
            across = jnp.maximum(across, jnp.where(good, some, 0.0))
    found = jnp.maximum(jnp.concatenate(found, axis=1), best_ref[...])
    turned = [jnp.transpose(across[at : at + LANES]) for at in range(0, dp_size * window, LANES)]
    across = jnp.concatenate([jnp.max(part, axis=0, keepdims=True) for part in turned], axis=1)
    for block in range(dp_size):
        parts = (found[:, block * half : (block + 1) * half], across[:, block * window : (block + 1) * window])
        out_ref[block] = jnp.broadcast_to(jnp.concatenate(parts, axis=1), (mp_size, half + window))


def pick_kernel(half, results_ref, target_ref, out_ref):
    device_count, length = results_ref.shape
    tiles = target_ref.shape[0]
    results = results_ref[:, :half]
    window = length - half
    if window:
        across = jnp.concatenate([results_ref[1:, half:], results_ref[:1, half:]], axis=0)
        across = jnp.concatenate([jnp.zeros((device_count, half - window), F32), across], axis=1)
        results = jnp.where(iota(results.shape, 0) % 2 == 0, jnp.maximum(results, across), results)
    high = results.astype(BF16)
    rest = results - high.astype(F32)
    middle = rest.astype(BF16)
    low = (rest - middle.astype(F32)).astype(BF16)
    pieces = jnp.concatenate([high, middle, low], axis=0)
    device_ids = iota((device_count, LANES), 0)
    rank_ids = iota((half, LANES), 0)
    for tile in range(tiles):
        target = target_ref[tile : tile + 1, :]
        device = target // half
        one_hot = to_bf16(device_ids == device)
        one_hot = jnp.concatenate([one_hot, one_hot, one_hot], axis=0)
        ranked = lax.dot_general(pieces, one_hot, (((0,), (0,)), ((), ())), preferred_element_type=F32)
        hit = rank_ids == target - device * half
        out_ref[tile : tile + 1, :] = jnp.sum(jnp.where(hit, ranked, 0.0), axis=0, keepdims=True)


def call(kernel, out_shape, specs, out_specs=None, scratch=(), cost=0, megabytes=32):
    return pl.pallas_call(
        kernel,
        out_shape=out_shape,
        in_specs=specs,
        out_specs=out_specs or jax.tree.map(lambda _: VMEM, out_shape),
        scratch_shapes=list(scratch),
        compiler_params=pltpu.CompilerParams(vmem_limit_bytes=megabytes << 20),
        cost_estimate=pl.CostEstimate(flops=cost, bytes_accessed=1 << 20, transcendentals=0),
    )


def routed(half, place, embeddings, sums, clusters, orders):
    shape = jax.ShapeDtypeStruct
    block_rows, features = embeddings.shape
    docs = clusters.shape[0] * LANES
    dp_size, mp_size = lax.axis_size("dp"), lax.axis_size("mp")
    devices = dp_size * mp_size
    tiles = block_rows // LANES
    slots = dp_size * half
    window = 2 * block_rows // devices - half
    targets, pair, loads = call(
        functools.partial(plan_kernel, dp_size, half),
        (shape((tiles, LANES), I32), *[shape((devices, LANES), F32)] * 2),
        [SMEM, VMEM],
        cost=10**8,
    )(place, clusters)
    size = max(size for size in range(LANES, 1281, LANES) if devices * half % size == 0)

    def whole(array):
        return pl.BlockSpec(array.shape, lambda step: (0, 0))

    packed = (embeddings, targets, *sums)
    outgoing = pl.pallas_call(
        pack_kernel,
        grid=(devices * half // size,),
        out_shape=shape((devices * half, features), BF16),
        in_specs=[whole(array) for array in packed],
        out_specs=pl.BlockSpec((size, features), lambda step: (step, 0)),
        scratch_shapes=[pltpu.VMEM((block_rows, features), BF16), pltpu.VMEM((size, block_rows), BF16)],
        compiler_params=pltpu.CompilerParams(vmem_limit_bytes=40 << 20),
    )(*packed)
    sources, outgoing = lax.optimization_barrier(((clusters, orders, pair), outgoing))
    arrived = lax.all_to_all(
        outgoing.reshape(devices, half, features), AXES, split_axis=0, concat_axis=0, tiled=True
    ).reshape(dp_size, mp_size, half, features)
    columns = [shape((dp_size * count, LANES), I32) for count in (half, window) if count]
    key_rows, own_columns, *window_columns = call(
        functools.partial(keys_kernel, dp_size, half, window, docs),
        (shape((slots // LANES, LANES), I32), *columns),
        [SMEM, VMEM, VMEM, VMEM],
        cost=10**9,
    )(place, *sources)
    fits = (jnp.max(loads) <= 2 * half).astype(I32)
    arrived, key_rows, fits = lax.optimization_barrier((arrived, key_rows, fits))
    work = 2 * slots * slots * features * mp_size
    best = call(
        functools.partial(own_pairs_kernel, docs),
        shape((1, slots) if window else (dp_size, mp_size, half), F32),
        [VMEM] * 3,
        cost=work,
    )(arrived, key_rows, own_columns)
    if window:
        other = lax.ppermute(arrived[:, :, half - window :], "mp", [(i, i ^ 1) for i in range(mp_size)])
        best = call(
            functools.partial(cross_pairs_kernel, docs),
            shape((dp_size, mp_size, half + window), F32),
            [VMEM] * 5,
            cost=work,
        )(arrived, other, key_rows, window_columns[0], best)
    results = lax.all_to_all(
        best.reshape(devices, half + window), AXES, split_axis=0, concat_axis=0, tiled=True
    )
    return results, targets, fits


def pick(half, results, targets):
    picked = call(
        functools.partial(pick_kernel, half), jax.ShapeDtypeStruct(targets.shape, F32), [VMEM, VMEM], cost=10**8
    )(results, targets)
    return picked.reshape(targets.size)


def shards(embeddings, cluster_of, doc_order):
    block_rows, _ = embeddings.shape
    docs = cluster_of.shape[0]
    mp_size = lax.axis_size("mp")
    devices = lax.axis_size("dp") * mp_size
    most = 2 * block_rows // devices
    half = -(-5 * most // 8 // 16) * 16
    dp_size = lax.axis_size("dp")
    if dp_size * half % LANES or dp_size * (most - half) % LANES:
        half = most
    dp_index, mp_index = lax.axis_index("dp"), lax.axis_index("mp")
    place = jnp.stack([dp_index, dp_index * mp_size + mp_index]).astype(I32)
    clusters = cluster_of.reshape(docs // LANES, LANES)
    orders = doc_order.reshape(docs // LANES, LANES)
    shape = jax.ShapeDtypeStruct
    squares, clusters, embeddings = pl.pallas_call(
        squares_kernel,
        out_shape=(
            shape((block_rows // LANES, LANES), F32),
            shape(clusters.shape, I32),
            shape(embeddings.shape, F32),
        ),
        in_specs=[pl.BlockSpec(memory_space=pltpu.HBM)] * 2,
        out_specs=(VMEM, VMEM, VMEM),
        scratch_shapes=[pltpu.SemaphoreType.DMA((5,))],
        compiler_params=pltpu.CompilerParams(vmem_limit_bytes=58 << 20),
    )(embeddings, clusters)
    others = [lax.ppermute(squares, "mp", [(i, i ^ k) for i in range(mp_size)]) for k in range(mp_size - 1, 0, -1)]
    sums = (squares, *others)
    arrays = (place, embeddings, sums, clusters, orders)
    results, targets, fits = routed(half, *arrays)
    if half == most:
        return pick(half, results, targets)
    return lax.cond(
        fits,
        lambda results, targets, *_: pick(half, results, targets),
        lambda _results, _targets, *rest: pick(most, *routed(most, *rest)[:2]),
        results,
        targets,
        *arrays,
    )


def solution(mesh):
    return jax.shard_map(
        shards,
        mesh=mesh,
        in_specs=(P("dp", "mp"), P(), P()),
        out_specs=P("dp"),
        check_vma=False,
    )
```
